32 devices in a mesh: groups: 2 (over x), ctx: 16 (over z, y, core).
Axes of the slice: x: 2, y: 2, z: 4, core: 2. Of those that a mesh axis runs over, the one named last changes fastest.
Arguments:
- query: bfloat16 [4096, 1536], P(('groups', 'ctx')), parts along dimension 0, may hold values from -5 to 5
- key_rows: bfloat16 [4096, 1536], P(('groups', 'ctx')), parts along dimension 0, may hold values from -5 to 5
- value: bfloat16 [4096, 1536], P(('groups', 'ctx')), parts along dimension 0, may hold values from -6 to 6
- grad_out: bfloat16 [4096, 1536], P(('groups', 'ctx')), parts along dimension 0, may hold values from -6 to 6
- kv_slots: int32 [16, 18], replicated, may hold values from -1 to 15, as said below
Outputs:
- out: bfloat16 [4096, 1536], P(('groups', 'ctx')), parts along dimension 0
- grad_query: bfloat16 [4096, 1536], P(('groups', 'ctx')), parts along dimension 0
- grad_key: bfloat16 [4096, 1536], P(('groups', 'ctx')), parts along dimension 0
- grad_value: bfloat16 [4096, 1536], P(('groups', 'ctx')), parts along dimension 0
The draws below stay inside these ranges and needn't reach their ends.
There are 2 independent parts, one for each index of `groups`. The reference program is written for one: setup_inputs(seed, part) draws one part's arguments, and reference() takes and returns one part's arrays. A program takes and returns all parts, laid end to end along the dimension named above; an argument that names none is the same for every part. Nothing has to cross between parts.
Inputs may be any that keep to these rules, and one draw needn't show every extreme that they name: `kv_slots`: blocks are the tiles of two time planes of 4 x 2 tiles in raster order (plane, row, column). The row of block b lists, in a drawn order, b itself and a drawn subset of the blocks whose tile lies in either plane within one row and one column of b's tile; -1 fills the other entries. No block is listed twice in a row.
All inputs are finite; a program needn't handle non-finite values.
Results may differ from the reference program's by a relative error of at most 0.0065.
The reference program's roundings to bfloat16 on the way (of `weights` and `grad_scores`) count: a program that leaves them out, or rounds other values in their place, can miss the bound.
Values may be sent and summed in bfloat16 or wider, within the bound.
A program may use at most 128 MiB of HBM per device.

```python
import jax
import jax.numpy as jnp
from jax import lax

HEADS = 12
HEAD = 128
BLOCK = 128
TILE_H = 4
KSLOT = 18
NBLK = 16
TOKENS = 2048
FEAT = 1536


def paired_fields(key):
    seeded = jax.random.fold_in(key, 11)
    first_key, second_key = jax.random.split(seeded, 2)
    features = HEADS * HEAD
    query_field = jnp.clip(jax.random.normal(first_key, (TOKENS, features), jnp.float32), -5.0, 5.0)
    key_field = jnp.clip(jax.random.normal(second_key, (TOKENS, features), jnp.float32), -5.0, 5.0)
    return (query_field, key_field)


def draw_query(key, part):
    return paired_fields(key)[0].astype(jnp.bfloat16)


def draw_key_rows(key, part):
    return paired_fields(key)[1].astype(jnp.bfloat16)


def draw_kv_slots(key, part):
    slot_ids = jnp.arange(NBLK, dtype=jnp.int32)
    tile_width = NBLK // (2 * TILE_H)
    plane_size = TILE_H * tile_width
    plane_of = slot_ids // plane_size
    row_of = slot_ids // tile_width % TILE_H
    column_of = slot_ids % tile_width
    columns_list = []
    for plane_step in (0, 1):
        for row_step in (-1, 0, 1):
            for col_step in (-1, 0, 1):
                other_plane = jnp.abs(plane_of - plane_step)
                row_new = row_of + row_step
                column_new = column_of + col_step
                inside = (row_new >= 0) & (row_new < TILE_H) & (column_new >= 0) & (column_new < tile_width)
                columns_list.append(jnp.where(inside, other_plane * plane_size + row_new * tile_width + column_new, -1))
    slot_table = jnp.stack(columns_list, axis=1).astype(jnp.int32)
    keep_draw = jax.random.randint(jax.random.fold_in(key, 5), (NBLK, KSLOT), 0, 4).astype(jnp.int32)
    is_self = (jnp.arange(KSLOT, dtype=jnp.int32) == 4)[None, :]
    keep = (keep_draw > 0) | is_self
    slot_table = jnp.where(keep, slot_table, -1).astype(jnp.int32)
    orders = jax.vmap(lambda row_key: jax.random.permutation(row_key, KSLOT))(jax.random.split(key, NBLK))
    return jnp.take_along_axis(slot_table, orders.astype(jnp.int32), axis=1).astype(jnp.int32)


def block_levels(own_key, extent, cuts, low, largest):
    def one(dim, parts):
        steps = jax.random.uniform(jax.random.fold_in(jax.random.fold_in(own_key, 6), dim), (parts,), jnp.float32, low / len(cuts), largest / len(cuts))
        return jnp.repeat(jnp.exp(steps), extent[dim] // parts).reshape((-1,) + (1,) * (len(extent) - dim - 1))

    factor_of = one(*cuts[0])
    for cut in cuts[1:]:
        factor_of = factor_of * one(*cut)
    return factor_of


def centred(own_key, dims, deviation, bound, pieces=(), held_as=jnp.bfloat16):
    array = deviation * jax.random.normal(own_key, dims, jnp.float32)
    if pieces:
        array = array * block_levels(own_key, dims, pieces, -0.22, 0.18)
    return jnp.clip(array, -bound, bound).astype(held_as)


def setup_inputs(seed: int = 0, part: int = 0) -> dict:
    seeds = jax.random.split(jax.random.key(seed), 6)
    part_splits = jax.random.split(jax.random.fold_in(seeds[5], part), 6)
    return {
        "query": draw_query(jax.random.fold_in(jax.random.fold_in(seeds[5], part), 71), part),
        "key_rows": draw_key_rows(jax.random.fold_in(jax.random.fold_in(seeds[5], part), 71), part),
        "value": centred(part_splits[2], (TOKENS, FEAT), 1.0, 6.0, ((0, 16),)),
        "grad_out": centred(part_splits[3], (TOKENS, FEAT), 1.0, 6.0, ((0, 16),)),
        "kv_slots": draw_kv_slots(jax.random.fold_in(seeds[5], 71), part),
    }


def block_scores(query_block, key_blocks, is_valid, scaling):
    scores = jnp.einsum("qhd,jkhd->hqjk", query_block.astype(jnp.float32), key_blocks.astype(jnp.float32)) * scaling
    return jnp.where(is_valid[None, None, :, None], scores, -1e30)


def reference(query, key_rows, value, grad_out, kv_slots):
    block_count = TOKENS // BLOCK
    query_blocks = query.reshape(block_count, BLOCK, HEADS, HEAD)
    key_blocks = key_rows.reshape(block_count, BLOCK, HEADS, HEAD)
    value_blocks = value.reshape(block_count, BLOCK, HEADS, HEAD)
    grad_blocks = grad_out.reshape(block_count, BLOCK, HEADS, HEAD)
    is_valid = kv_slots >= 0
    safe_slot = jnp.where(is_valid, kv_slots, 0).astype(jnp.int32)
    scaling = HEAD ** -0.5

    def forward(block_index):
        keys_here = key_blocks[safe_slot[block_index]]
        values_here = value_blocks[safe_slot[block_index]]
        scores = block_scores(query_blocks[block_index], keys_here, is_valid[block_index], scaling)
        peak_score = jnp.max(scores, axis=(2, 3), keepdims=True)
        log_norm = peak_score + jnp.log(jnp.sum(jnp.exp(scores - peak_score), axis=(2, 3), keepdims=True))
        weights = lax.optimization_barrier(jnp.exp(scores - log_norm).astype(jnp.bfloat16))
        mixed_rows = jnp.einsum("hqjk,jkhd->qhd", weights.astype(jnp.float32), values_here.astype(jnp.float32))
        return mixed_rows.astype(jnp.bfloat16), log_norm[:, :, 0, 0]

    out_blocks, log_norms = lax.map(forward, jnp.arange(block_count))
    delta_rows = jnp.sum(grad_blocks.astype(jnp.float32) * out_blocks.astype(jnp.float32), axis=3)

    def backward(carry, block_index):
        key_total, value_total = carry
        keys_here = key_blocks[safe_slot[block_index]]
        values_here = value_blocks[safe_slot[block_index]]
        scores = block_scores(query_blocks[block_index], keys_here, is_valid[block_index], scaling)
        weights = jnp.exp(scores - log_norms[block_index][:, :, None, None])
        weights_low = lax.optimization_barrier(weights.astype(jnp.bfloat16))
        grad_here = grad_blocks[block_index].astype(jnp.float32)
        grad_probs = jnp.einsum("qhd,jkhd->hqjk", grad_here, values_here.astype(jnp.float32))
        grad_scores = weights * (grad_probs - jnp.transpose(delta_rows[block_index])[:, :, None, None])
        grad_scores = lax.optimization_barrier(grad_scores.astype(jnp.bfloat16)).astype(jnp.float32)
        grad_query_block = (jnp.einsum("hqjk,jkhd->qhd", grad_scores, keys_here.astype(jnp.float32)) * scaling).astype(jnp.bfloat16)
        value_part = jnp.einsum("hqjk,qhd->jkhd", weights_low.astype(jnp.float32), grad_here)
        key_part = jnp.einsum("hqjk,qhd->jkhd", grad_scores, query_blocks[block_index].astype(jnp.float32)) * scaling
        keep = is_valid[block_index][:, None, None, None]
        key_total = key_total.at[safe_slot[block_index]].add(jnp.where(keep, key_part, 0.0))
        value_total = value_total.at[safe_slot[block_index]].add(jnp.where(keep, value_part, 0.0))
        return (key_total, value_total), grad_query_block

    zero_blocks = jnp.zeros((block_count, BLOCK, HEADS, HEAD), jnp.float32)
    (key_total, value_total), grad_query_blocks = lax.scan(backward, (zero_blocks, zero_blocks), jnp.arange(block_count))
    features = HEADS * HEAD
    return (out_blocks.reshape(TOKENS, features),
            grad_query_blocks.reshape(TOKENS, features),
            key_total.astype(jnp.bfloat16).reshape(TOKENS, features),
            value_total.astype(jnp.bfloat16).reshape(TOKENS, features))
```

```python
import functools

import jax
import jax.numpy as jnp
from jax import lax
from jax.experimental import pallas as pl
from jax.experimental.pallas import tpu as pltpu
from jax.sharding import PartitionSpec as P

HEADS = 12
HEAD = 128
BLOCK = 128
TILE_H = 4


head_batch = 4
masked_score = -1e30
VMEM_BYTES = 48 * 1024 * 1024


def from_behind(value, axis, by):
    count = lax.axis_size(axis)
    return lax.ppermute(value, axis, [(i, (i + by) % count) for i in range(count)])


def neighbour_offsets(devices, blocks, tile_width):
    plane_size = TILE_H * tile_width
    total_slots = devices * blocks
    offset_set = set()
    for plane_step in (0, 1):
        for row_step in (-1, 0, 1):
            for col_step in (-1, 0, 1):
                offset = (plane_step * plane_size + row_step * tile_width + col_step) % total_slots
                target = offset % total_slots // blocks
                if target > devices // 2:
                    target = target - devices
                if target != 0:
                    offset_set.add(target)
    return offset_set


def split_heads(tensor):
    return tensor.reshape(
        tensor.shape[0], HEADS // head_batch, head_batch, tensor.shape[1] // HEADS
    )


def pick_group(tensor, group_index):
    return lax.dynamic_index_in_dim(tensor, group_index, 1, keepdims=False)


def join_heads(stacked):
    return jnp.moveaxis(stacked, 0, 1).reshape(stacked.shape[1], -1)


def apply_mask(scores, block_mask):
    heads_here, row_total, col_total = scores.shape
    row_blocks, col_blocks = block_mask.shape
    shaped = scores.reshape(
        heads_here, row_blocks, row_total // row_blocks, col_blocks, col_total // col_blocks
    )
    shaped = jnp.where(block_mask[None, :, None, :, None], shaped, masked_score)
    return shaped.reshape(heads_here, row_total, col_total)


def forward_group(group_index, queries, keys, values, allowed, scaling):
    query_part = pick_group(queries, group_index)
    key_part = pick_group(keys, group_index)
    value_part = pick_group(values, group_index)
    scores = (
        jnp.einsum("qhd,khd->hqk", query_part, key_part, preferred_element_type=jnp.float32)
        * scaling
    )
    scores = apply_mask(scores, allowed)
    peak_score = jnp.max(scores, axis=2, keepdims=True)
    denominator = jnp.sum(jnp.exp(scores - peak_score), axis=2, keepdims=True)
    log_norm = peak_score + jnp.log(denominator)
    weights = jnp.exp(scores - log_norm).astype(jnp.bfloat16)
    mixed_rows = jnp.einsum("hqk,khd->qhd", weights, value_part, preferred_element_type=jnp.float32)
    return (mixed_rows, log_norm[:, :, 0])


def query_group(
    group_index, queries, keys, values, gradients, log_split, delta_split, allowed, scaling
):
    query_part = pick_group(queries, group_index)
    key_part = pick_group(keys, group_index)
    value_part = pick_group(values, group_index)
    grad_part = pick_group(gradients, group_index)
    log_part = jnp.transpose(pick_group(log_split, group_index))
    delta_part = jnp.transpose(pick_group(delta_split, group_index))
    scores = (
        jnp.einsum("qhd,khd->hqk", query_part, key_part, preferred_element_type=jnp.float32)
        * scaling
    )
    scores = apply_mask(scores, allowed)
    weights = jnp.exp(scores - log_part[:, :, None])
    grad_probs = jnp.einsum(
        "qhd,khd->hqk", grad_part, value_part, preferred_element_type=jnp.float32
    )
    grad_scores = (weights * (grad_probs - delta_part[:, :, None])).astype(jnp.bfloat16)
    return (
        jnp.einsum("hqk,khd->qhd", grad_scores, key_part, preferred_element_type=jnp.float32)
        * scaling
    )


def key_group(
    group_index, keys, values, queries, gradients, log_split, delta_split, back_mask, scaling
):
    key_part = pick_group(keys, group_index)
    value_part = pick_group(values, group_index)
    query_part = pick_group(queries, group_index)
    grad_part = pick_group(gradients, group_index)
    log_part = jnp.transpose(pick_group(log_split, group_index))
    delta_part = jnp.transpose(pick_group(delta_split, group_index))
    scores = (
        jnp.einsum("khd,chd->hkc", key_part, query_part, preferred_element_type=jnp.float32)
        * scaling
    )
    scores = apply_mask(scores, back_mask)
    weights = jnp.exp(scores - log_part[:, None, :])
    grad_probs = jnp.einsum(
        "khd,chd->hkc", value_part, grad_part, preferred_element_type=jnp.float32
    )
    grad_scores = (weights * (grad_probs - delta_part[:, None, :])).astype(jnp.bfloat16)
    grad_values = jnp.einsum(
        "hkc,chd->khd", weights.astype(jnp.bfloat16), grad_part, preferred_element_type=jnp.float32
    )
    grad_keys = (
        jnp.einsum("hkc,chd->khd", grad_scores, query_part, preferred_element_type=jnp.float32)
        * scaling
    )
    return (grad_keys, grad_values)


def body(query, key_rows, value, grad_out, kv_slots):
    devices = lax.axis_size("ctx")
    device_index = lax.axis_index("ctx")
    row_count = query.shape[0]
    blocks = row_count // BLOCK
    tile_width = devices * blocks // (2 * TILE_H)
    offset_set = neighbour_offsets(devices, blocks, tile_width)
    visit_order = sorted(offset_set)
    distances = [0] + visit_order
    local_slots = jnp.arange(blocks, dtype=jnp.int32)
    cand_slots = jnp.concatenate(
        [(device_index + distance) % devices * blocks + local_slots for distance in distances]
    ).astype(jnp.int32)
    own_blocks = device_index * blocks + local_slots
    own_lists = lax.dynamic_slice_in_dim(kv_slots, device_index * blocks, blocks, 0)
    allowed = jnp.any(own_lists[:, :, None] == cand_slots[None, None, :], axis=1)
    cand_lists = jnp.take(kv_slots, cand_slots, axis=0)
    back_mask = jnp.any(cand_lists[None, :, :] == own_blocks[:, None, None], axis=2)
    scaling = HEAD ** (-0.5)
    groups = HEADS // head_batch
    group_ids = jnp.arange(groups)
    arrived = [from_behind((key_rows, value), "ctx", -distance) for distance in visit_order]
    cand_keys = split_heads(jnp.concatenate([key_rows] + [item[0] for item in arrived], axis=0))
    cand_values = split_heads(jnp.concatenate([value] + [item[1] for item in arrived], axis=0))
    queries = split_heads(query)
    mixed_all, norm_all = lax.map(
        lambda group_index: forward_group(
            group_index, queries, cand_keys, cand_values, allowed, scaling
        ),
        group_ids,
    )
    out = join_heads(mixed_all).astype(jnp.bfloat16)
    log_rows = jnp.transpose(norm_all.reshape(HEADS, row_count))
    delta_rows = jnp.sum(
        (grad_out.astype(jnp.float32) * out.astype(jnp.float32)).reshape(row_count, HEADS, -1),
        axis=2,
    )
    gradients = split_heads(grad_out)
    log_split = log_rows.reshape(row_count, groups, head_batch)
    delta_split = delta_rows.reshape(row_count, groups, head_batch)
    query_terms = lax.map(
        lambda group_index: query_group(
            group_index,
            queries,
            cand_keys,
            cand_values,
            gradients,
            log_split,
            delta_split,
            allowed,
            scaling,
        ),
        group_ids,
    )
    grad_query = join_heads(query_terms).astype(jnp.bfloat16)
    returned = [from_behind((query, grad_out), "ctx", -distance) for distance in visit_order]
    cand_queries = jnp.concatenate([query] + [item[0] for item in returned], axis=0)
    cand_grads = jnp.concatenate([grad_out] + [item[1] for item in returned], axis=0)
    row_terms = [from_behind((log_rows, delta_rows), "ctx", -distance) for distance in visit_order]
    cand_log = jnp.concatenate([log_rows] + [item[0] for item in row_terms], axis=0).reshape(
        -1, groups, head_batch
    )
    cand_delta = jnp.concatenate([delta_rows] + [item[1] for item in row_terms], axis=0).reshape(
        -1, groups, head_batch
    )
    own_keys = split_heads(key_rows)
    own_values = split_heads(value)
    split_queries = split_heads(cand_queries)
    split_grads = split_heads(cand_grads)
    key_terms, value_terms = lax.map(
        lambda group_index: key_group(
            group_index,
            own_keys,
            own_values,
            split_queries,
            split_grads,
            cand_log,
            cand_delta,
            back_mask,
            scaling,
        ),
        group_ids,
    )
    grad_key = join_heads(key_terms).astype(jnp.bfloat16)
    grad_value = join_heads(value_terms).astype(jnp.bfloat16)
    return (out, grad_query, grad_key, grad_value)


def head_owner(head, devices):
    chips = devices // 2
    first = (chips - (HEADS - chips)) // 2
    return jnp.where(head < chips, 2 * head, 2 * (head - chips + first) + 1)


def head_of(device, devices):
    chips = devices // 2
    extra = HEADS - chips
    first = (chips - extra) // 2
    chip = device // 2
    odd = device % 2
    inside = (chip >= first) & (chip < first + extra)
    second = jnp.where(inside, chips + chip - first, -1)
    return jnp.where(odd == 0, jnp.where(chip < HEADS, chip, -1), second)


def exchange_kernel(
    devices,
    query_ref,
    key_ref,
    value_ref,
    grad_ref,
    slots_ref,
    out_ref,
    dq_ref,
    dk_ref,
    dv_ref,
    q_all,
    k_all,
    v_all,
    g_all,
    kt_all,
    vt_all,
    gt_all,
    ot_all,
    o_all,
    dq_all,
    dk_all,
    dv_all,
    dk_sum,
    dv_sum,
    bias,
    probs,
    in_send,
    in_recv,
    out_send,
    out_recv,
):
    me = lax.axis_index("ctx")
    my_head = head_of(me, devices)
    owns = my_head >= 0
    tokens = devices * BLOCK
    width = devices // (2 * TILE_H)
    row_tokens = width * BLOCK
    plane_tokens = tokens // 2
    scaling = HEAD ** (-0.5)

    barrier = pltpu.get_barrier_semaphore()
    for step in range(1, devices):
        pl.semaphore_signal(
            barrier,
            inc=1,
            device_id={"ctx": lax.rem(me + step, devices)},
            device_id_type=pl.DeviceIdType.MESH,
        )
    pl.semaphore_wait(barrier, devices - 1)

    sources = (key_ref, query_ref, value_ref, grad_ref)
    landings = (k_all, q_all, v_all, g_all)
    own_rows = pl.ds(pl.multiple_of(me * BLOCK, BLOCK), BLOCK)

    def send_inputs(index):
        source, landing = sources[index], landings[index]

        def one(step, carry):
            head = lax.rem(me + step, HEADS)
            owner = head_owner(head, devices)
            columns = pl.ds(pl.multiple_of(head * HEAD, HEAD), HEAD)

            @pl.when(owner != me)
            def _():
                pltpu.make_async_remote_copy(
                    src_ref=source.at[:, columns],
                    dst_ref=landing.at[own_rows, :],
                    send_sem=in_send.at[index],
                    recv_sem=in_recv.at[index],
                    device_id={"ctx": owner},
                    device_id_type=pl.DeviceIdType.MESH,
                ).start()

            @pl.when(owner == me)
            def _():
                pltpu.make_async_copy(
                    source.at[:, columns], landing.at[own_rows, :], in_recv.at[index]
                ).start()

            return carry

        lax.fori_loop(0, HEADS, one, 0)

    for index in range(4):
        send_inputs(index)

    def arrived(index):
        pltpu.make_async_copy(landings[index], landings[index], in_recv.at[index]).wait()

    results = (o_all, dq_all, dk_all, dv_all)
    targets = (out_ref, dq_ref, dk_ref, dv_ref)

    def send_results(index):
        result, target = results[index], targets[index]
        columns = pl.ds(pl.multiple_of(my_head * HEAD, HEAD), HEAD)

        def one(step, carry):
            other = lax.rem(me + step, devices)
            rows = pl.ds(pl.multiple_of(other * BLOCK, BLOCK), BLOCK)
            pltpu.make_async_remote_copy(
                src_ref=result.at[rows, :],
                dst_ref=target.at[:, columns],
                send_sem=out_send.at[index],
                recv_sem=out_recv.at[index],
                device_id={"ctx": other},
                device_id_type=pl.DeviceIdType.MESH,
            ).start()
            return carry

        lax.fori_loop(1, devices, one, 0)
        pltpu.make_async_copy(
            result.at[own_rows, :], target.at[:, columns], out_recv.at[index]
        ).start()

    def dot(left, right):
        return jnp.dot(left, right, preferred_element_type=jnp.float32)

    def dot_nt(left, right):
        return lax.dot_general(
            left, right, (((1,), (1,)), ((), ())), preferred_element_type=jnp.float32
        )

    def flip(ref, target):
        for start in range(0, tokens, row_tokens):
            part = ref[start : start + row_tokens, :].astype(jnp.float32)
            target[:, start : start + row_tokens] = jnp.transpose(part).astype(target.dtype)

    groups = []
    for row in range(TILE_H):
        low, high = max(row - 1, 0), min(row + 1, TILE_H - 1)
        count = (high + 1 - low) * row_tokens
        for plane in range(2):
            groups.append(
                (
                    plane * plane_tokens + row * row_tokens,
                    [(0, low * row_tokens), (count, plane_tokens + low * row_tokens)],
                    count,
                )
            )

    @pl.when(owns)
    def _():
        for block in range(devices):
            listed = slots_ref[block : block + 1, :]
            ids = lax.broadcasted_iota(jnp.int32, (devices, listed.shape[1]), 0)
            hit = jnp.where(ids == listed, 0.0, -1e30)
            best = jnp.max(hit, axis=1, keepdims=True)
            bias[:, block * BLOCK : (block + 1) * BLOCK] = jnp.broadcast_to(best, (devices, BLOCK))
        dk_sum[...] = jnp.zeros_like(dk_sum)
        dv_sum[...] = jnp.zeros_like(dv_sum)

        arrived(0)
        arrived(1)
        flip(k_all, kt_all)
        for index, (start, ranges, count) in enumerate(groups):
            queries = q_all[start : start + row_tokens, :]
            scores = []
            for offset, first in ranges:
                part = dot_nt(k_all[first : first + count, :], queries) * scaling
                blocks = count // BLOCK
                shift = bias[first // BLOCK : first // BLOCK + blocks, start : start + row_tokens]
                part = part.reshape(blocks, BLOCK, row_tokens) + shift[:, None, :]
                scores.append(part.reshape(count, row_tokens))
            peak = jnp.maximum(
                jnp.max(scores[0], axis=0, keepdims=True), jnp.max(scores[1], axis=0, keepdims=True)
            )
            powers = [jnp.exp(part - peak) for part in scores]
            total = jnp.sum(powers[0], axis=0, keepdims=True) + jnp.sum(
                powers[1], axis=0, keepdims=True
            )
            inverse = 1.0 / total
            for (offset, first), part in zip(ranges, powers):
                probs[index, offset : offset + count, :] = part * inverse

        arrived(2)
        flip(v_all, vt_all)
        for index, (start, ranges, count) in enumerate(groups):
            mixed = jnp.zeros((HEAD, row_tokens), jnp.float32)
            for offset, first in ranges:
                weights = probs[index, offset : offset + count, :].astype(jnp.bfloat16)
                mixed += dot(vt_all[:, first : first + count], weights)
            ot_all[:, start : start + row_tokens] = mixed.astype(jnp.bfloat16)
            o_all[start : start + row_tokens, :] = jnp.transpose(mixed).astype(jnp.bfloat16)
        send_results(0)

        arrived(3)
        flip(g_all, gt_all)
        for index, (start, ranges, count) in enumerate(groups):
            span = slice(start, start + row_tokens)
            delta = jnp.sum(
                gt_all[:, span].astype(jnp.float32) * ot_all[:, span].astype(jnp.float32),
                axis=0,
                keepdims=True,
            )
            grads = g_all[span, :]
            queries = q_all[span, :]
            turned = jnp.zeros((HEAD, row_tokens), jnp.float32)
            for offset, first in ranges:
                keys = slice(first, first + count)
                exact = probs[index, offset : offset + count, :]
                dv_sum[keys, :] += dot(exact.astype(jnp.bfloat16), grads)
                product = dot_nt(v_all[keys, :], grads)
                slopes = (exact * (product - delta)).astype(jnp.bfloat16)
                turned += dot(kt_all[:, keys], slopes)
                dk_sum[keys, :] += dot(slopes, queries)
            dq_all[span, :] = jnp.transpose(turned * scaling).astype(jnp.bfloat16)
        dv_all[...] = dv_sum[...].astype(jnp.bfloat16)
        send_results(3)
        dk_all[...] = (dk_sum[...] * scaling).astype(jnp.bfloat16)
        send_results(2)
        send_results(1)

        for index in range(4):
            sent = sources[index].at[:, : (HEADS - 1) * HEAD]
            pltpu.make_async_copy(sent, sent, in_send.at[index]).wait()
            sent = results[index].at[: (devices - 1) * BLOCK, :]
            pltpu.make_async_copy(sent, sent, out_send.at[index]).wait()

    @pl.when(jnp.logical_not(owns))
    def _():
        for index in range(4):
            pltpu.make_async_copy(sources[index], sources[index], in_send.at[index]).wait()

    for index in range(4):
        pltpu.make_async_copy(targets[index], targets[index], out_recv.at[index]).wait()


def exchange_sizes(devices):
    tokens = devices * BLOCK
    row_tokens = tokens // (2 * TILE_H)
    return tokens, (2 * TILE_H, 6 * row_tokens, row_tokens)


def exchange_body(query, key_rows, value, grad_out, kv_slots):
    devices = lax.axis_size("ctx")
    tokens, probs_shape = exchange_sizes(devices)
    low = lambda *shape: pltpu.VMEM(shape, jnp.bfloat16)
    full = lambda *shape: pltpu.VMEM(shape, jnp.float32)
    anywhere = pl.BlockSpec(memory_space=pl.ANY)
    whole = jax.ShapeDtypeStruct(query.shape, query.dtype)
    return pl.pallas_call(
        functools.partial(exchange_kernel, devices),
        out_shape=(whole,) * 4,
        in_specs=[anywhere] * 4 + [pl.BlockSpec(memory_space=pltpu.VMEM)],
        out_specs=(anywhere,) * 4,
        scratch_shapes=[low(tokens, HEAD)] * 4
        + [low(HEAD, tokens)] * 4
        + [low(tokens, HEAD)] * 4
        + [full(tokens, HEAD)] * 2
        + [full(devices, tokens), full(*probs_shape)]
        + [pltpu.SemaphoreType.DMA((4,))] * 4,
        compiler_params=pltpu.CompilerParams(
            collective_id=0, has_side_effects=True, vmem_limit_bytes=VMEM_BYTES
        ),
    )(query, key_rows, value, grad_out, kv_slots)


def fits_exchange(devices, rows):
    if rows != devices * BLOCK or devices % (2 * TILE_H) or not devices // 2 <= HEADS <= devices:
        return False
    _, (groups, keys, queries) = exchange_sizes(devices)
    return groups * keys * queries * 4 <= VMEM_BYTES // 2


def solution(mesh):
    placed = P(("groups", "ctx"), None)

    def chosen(query, key_rows, value, grad_out, kv_slots):
        devices = mesh.shape["ctx"]
        rows = query.shape[0] // mesh.shape["groups"]
        return jax.shard_map(
            exchange_body if fits_exchange(devices, rows) else body,
            mesh=mesh,
            in_specs=(placed,) * 4 + (P(),),
            out_specs=(placed,) * 4,
            check_vma=False,
        )(query, key_rows, value, grad_out, kv_slots)

    return chosen
```

```python
import functools

import jax
import jax.numpy as jnp
from jax import lax
from jax.experimental import pallas as pl
from jax.experimental.pallas import tpu as pltpu
from jax.sharding import PartitionSpec as P

HEADS = 12
HEAD = 128
BLOCK = 128
TILE_H = 4


head_batch = 4
masked_score = -1e30
VMEM_BYTES = 63 * 1024 * 1024


def from_behind(value, axis, by):
    count = lax.axis_size(axis)
    return lax.ppermute(value, axis, [(i, (i + by) % count) for i in range(count)])


def neighbour_offsets(devices, blocks, tile_width):
    plane_size = TILE_H * tile_width
    total_slots = devices * blocks
    offset_set = set()
    for plane_step in (0, 1):
        for row_step in (-1, 0, 1):
            for col_step in (-1, 0, 1):
                offset = (plane_step * plane_size + row_step * tile_width + col_step) % total_slots
                target = offset % total_slots // blocks
                if target > devices // 2:
                    target = target - devices
                if target != 0:
                    offset_set.add(target)
    return offset_set


def split_heads(tensor):
    return tensor.reshape(
        tensor.shape[0], HEADS // head_batch, head_batch, tensor.shape[1] // HEADS
    )


def pick_group(tensor, group_index):
    return lax.dynamic_index_in_dim(tensor, group_index, 1, keepdims=False)


def join_heads(stacked):
    return jnp.moveaxis(stacked, 0, 1).reshape(stacked.shape[1], -1)


def apply_mask(scores, block_mask):
    heads_here, row_total, col_total = scores.shape
    row_blocks, col_blocks = block_mask.shape
    shaped = scores.reshape(
        heads_here, row_blocks, row_total // row_blocks, col_blocks, col_total // col_blocks
    )
    shaped = jnp.where(block_mask[None, :, None, :, None], shaped, masked_score)
    return shaped.reshape(heads_here, row_total, col_total)


def forward_group(group_index, queries, keys, values, allowed, scaling):
    query_part = pick_group(queries, group_index)
    key_part = pick_group(keys, group_index)
    value_part = pick_group(values, group_index)
    scores = (
        jnp.einsum("qhd,khd->hqk", query_part, key_part, preferred_element_type=jnp.float32)
        * scaling
    )
    scores = apply_mask(scores, allowed)
    peak_score = jnp.max(scores, axis=2, keepdims=True)
    denominator = jnp.sum(jnp.exp(scores - peak_score), axis=2, keepdims=True)
    log_norm = peak_score + jnp.log(denominator)
    weights = jnp.exp(scores - log_norm).astype(jnp.bfloat16)
    mixed_rows = jnp.einsum("hqk,khd->qhd", weights, value_part, preferred_element_type=jnp.float32)
    return (mixed_rows, log_norm[:, :, 0])


def query_group(
    group_index, queries, keys, values, gradients, log_split, delta_split, allowed, scaling
):
    query_part = pick_group(queries, group_index)
    key_part = pick_group(keys, group_index)
    value_part = pick_group(values, group_index)
    grad_part = pick_group(gradients, group_index)
    log_part = jnp.transpose(pick_group(log_split, group_index))
    delta_part = jnp.transpose(pick_group(delta_split, group_index))
    scores = (
        jnp.einsum("qhd,khd->hqk", query_part, key_part, preferred_element_type=jnp.float32)
        * scaling
    )
    scores = apply_mask(scores, allowed)
    weights = jnp.exp(scores - log_part[:, :, None])
    grad_probs = jnp.einsum(
        "qhd,khd->hqk", grad_part, value_part, preferred_element_type=jnp.float32
    )
    grad_scores = (weights * (grad_probs - delta_part[:, :, None])).astype(jnp.bfloat16)
    return (
        jnp.einsum("hqk,khd->qhd", grad_scores, key_part, preferred_element_type=jnp.float32)
        * scaling
    )


def key_group(
    group_index, keys, values, queries, gradients, log_split, delta_split, back_mask, scaling
):
    key_part = pick_group(keys, group_index)
    value_part = pick_group(values, group_index)
    query_part = pick_group(queries, group_index)
    grad_part = pick_group(gradients, group_index)
    log_part = jnp.transpose(pick_group(log_split, group_index))
    delta_part = jnp.transpose(pick_group(delta_split, group_index))
    scores = (
        jnp.einsum("khd,chd->hkc", key_part, query_part, preferred_element_type=jnp.float32)
        * scaling
    )
    scores = apply_mask(scores, back_mask)
    weights = jnp.exp(scores - log_part[:, None, :])
    grad_probs = jnp.einsum(
        "khd,chd->hkc", value_part, grad_part, preferred_element_type=jnp.float32
    )
    grad_scores = (weights * (grad_probs - delta_part[:, None, :])).astype(jnp.bfloat16)
    grad_values = jnp.einsum(
        "hkc,chd->khd", weights.astype(jnp.bfloat16), grad_part, preferred_element_type=jnp.float32
    )
    grad_keys = (
        jnp.einsum("hkc,chd->khd", grad_scores, query_part, preferred_element_type=jnp.float32)
        * scaling
    )
    return (grad_keys, grad_values)


def body(query, key_rows, value, grad_out, kv_slots):
    devices = lax.axis_size("ctx")
    device_index = lax.axis_index("ctx")
    row_count = query.shape[0]
    blocks = row_count // BLOCK
    tile_width = devices * blocks // (2 * TILE_H)
    offset_set = neighbour_offsets(devices, blocks, tile_width)
    visit_order = sorted(offset_set)
    distances = [0] + visit_order
    local_slots = jnp.arange(blocks, dtype=jnp.int32)
    cand_slots = jnp.concatenate(
        [(device_index + distance) % devices * blocks + local_slots for distance in distances]
    ).astype(jnp.int32)
    own_blocks = device_index * blocks + local_slots
    own_lists = lax.dynamic_slice_in_dim(kv_slots, device_index * blocks, blocks, 0)
    allowed = jnp.any(own_lists[:, :, None] == cand_slots[None, None, :], axis=1)
    cand_lists = jnp.take(kv_slots, cand_slots, axis=0)
    back_mask = jnp.any(cand_lists[None, :, :] == own_blocks[:, None, None], axis=2)
    scaling = HEAD ** (-0.5)
    groups = HEADS // head_batch
    group_ids = jnp.arange(groups)
    arrived = [from_behind((key_rows, value), "ctx", -distance) for distance in visit_order]
    cand_keys = split_heads(jnp.concatenate([key_rows] + [item[0] for item in arrived], axis=0))
    cand_values = split_heads(jnp.concatenate([value] + [item[1] for item in arrived], axis=0))
    queries = split_heads(query)
    mixed_all, norm_all = lax.map(
        lambda group_index: forward_group(
            group_index, queries, cand_keys, cand_values, allowed, scaling
        ),
        group_ids,
    )
    out = join_heads(mixed_all).astype(jnp.bfloat16)
    log_rows = jnp.transpose(norm_all.reshape(HEADS, row_count))
    delta_rows = jnp.sum(
        (grad_out.astype(jnp.float32) * out.astype(jnp.float32)).reshape(row_count, HEADS, -1),
        axis=2,
    )
    gradients = split_heads(grad_out)
    log_split = log_rows.reshape(row_count, groups, head_batch)
    delta_split = delta_rows.reshape(row_count, groups, head_batch)
    query_terms = lax.map(
        lambda group_index: query_group(
            group_index,
            queries,
            cand_keys,
            cand_values,
            gradients,
            log_split,
            delta_split,
            allowed,
            scaling,
        ),
        group_ids,
    )
    grad_query = join_heads(query_terms).astype(jnp.bfloat16)
    returned = [from_behind((query, grad_out), "ctx", -distance) for distance in visit_order]
    cand_queries = jnp.concatenate([query] + [item[0] for item in returned], axis=0)
    cand_grads = jnp.concatenate([grad_out] + [item[1] for item in returned], axis=0)
    row_terms = [from_behind((log_rows, delta_rows), "ctx", -distance) for distance in visit_order]
    cand_log = jnp.concatenate([log_rows] + [item[0] for item in row_terms], axis=0).reshape(
        -1, groups, head_batch
    )
    cand_delta = jnp.concatenate([delta_rows] + [item[1] for item in row_terms], axis=0).reshape(
        -1, groups, head_batch
    )
    own_keys = split_heads(key_rows)
    own_values = split_heads(value)
    split_queries = split_heads(cand_queries)
    split_grads = split_heads(cand_grads)
    key_terms, value_terms = lax.map(
        lambda group_index: key_group(
            group_index,
            own_keys,
            own_values,
            split_queries,
            split_grads,
            cand_log,
            cand_delta,
            back_mask,
            scaling,
        ),
        group_ids,
    )
    grad_key = join_heads(key_terms).astype(jnp.bfloat16)
    grad_value = join_heads(value_terms).astype(jnp.bfloat16)
    return (out, grad_query, grad_key, grad_value)


def head_owner(head, devices):
    chips = devices // 2
    first = (chips - (HEADS - chips)) // 2
    return jnp.where(head < chips, 2 * head, 2 * (head - chips + first) + 1)


def head_of(device, devices):
    chips = devices // 2
    extra = HEADS - chips
    first = (chips - extra) // 2
    chip = device // 2
    odd = device % 2
    inside = (chip >= first) & (chip < first + extra)
    second = jnp.where(inside, chips + chip - first, -1)
    return jnp.where(odd == 0, jnp.where(chip < HEADS, chip, -1), second)


def exchange_kernel(
    devices,
    query_ref,
    key_ref,
    value_ref,
    grad_ref,
    slots_ref,
    out_ref,
    dq_ref,
    dk_ref,
    dv_ref,
    q_all,
    k_all,
    v_all,
    g_all,
    kt_all,
    vt_all,
    gt_all,
    ot_all,
    o_all,
    dq_all,
    dk_all,
    dv_all,
    dk_sum,
    dv_sum,
    bias,
    probs,
    in_send,
    in_recv,
    out_send,
    out_recv,
):
    me = lax.axis_index("ctx")
    my_head = head_of(me, devices)
    owns = my_head >= 0
    tokens = devices * BLOCK
    width = devices // (2 * TILE_H)
    row_tokens = width * BLOCK
    plane_tokens = tokens // 2
    scaling = HEAD ** (-0.5)

    barrier = pltpu.get_barrier_semaphore()
    for step in range(1, devices):
        pl.semaphore_signal(
            barrier,
            inc=1,
            device_id={"ctx": lax.rem(me + step, devices)},
            device_id_type=pl.DeviceIdType.MESH,
        )
    pl.semaphore_wait(barrier, devices - 1)

    sources = (key_ref, query_ref, value_ref, grad_ref)
    landings = (k_all, q_all, v_all, g_all)
    own_rows = pl.ds(pl.multiple_of(me * BLOCK, BLOCK), BLOCK)

    half = me // (devices // 2)
    chips = devices // 2
    pairs = HEADS // 2

    def send_inputs(index):
        source, landing = sources[index], landings[index]

        def one(step, carry):
            place = lax.rem(me + step, pairs)
            for side in (1 - half, half):
                head = jnp.where(
                    place < chips // 2,
                    place + side * (chips // 2),
                    chips + place - chips // 2 + side * ((HEADS - chips) // 2),
                )
                owner = head_owner(head, devices)
                columns = pl.ds(pl.multiple_of(head * HEAD, HEAD), HEAD)

                @pl.when(owner != me)
                def _():
                    pltpu.make_async_remote_copy(
                        src_ref=source.at[:, columns],
                        dst_ref=landing.at[own_rows, :],
                        send_sem=in_send.at[index],
                        recv_sem=in_recv.at[index],
                        device_id={"ctx": owner},
                        device_id_type=pl.DeviceIdType.MESH,
                    ).start()

                @pl.when(owner == me)
                def _():
                    pltpu.make_async_copy(
                        source.at[:, columns], landing.at[own_rows, :], in_recv.at[index]
                    ).start()

            return carry

        lax.fori_loop(0, pairs, one, 0)

    for index in range(4):
        send_inputs(index)

    def arrived(index):
        pltpu.make_async_copy(landings[index], landings[index], in_recv.at[index]).wait()

    results = (o_all, dq_all, dk_all, dv_all)
    targets = (out_ref, dq_ref, dk_ref, dv_ref)

    def send_row(index, row):
        result, target = results[index], targets[index]
        columns = pl.ds(pl.multiple_of(my_head * HEAD, HEAD), HEAD)
        for column in range(width):
            for side in (1 - half, half):
                other = side * (devices // 2) + row * width + column
                rows = pl.ds(pl.multiple_of(other * BLOCK, BLOCK), BLOCK)

                @pl.when(other != me)
                def _():
                    pltpu.make_async_remote_copy(
                        src_ref=result.at[rows, :],
                        dst_ref=target.at[:, columns],
                        send_sem=out_send.at[index],
                        recv_sem=out_recv.at[index],
                        device_id={"ctx": other},
                        device_id_type=pl.DeviceIdType.MESH,
                    ).start()

                @pl.when(other == me)
                def _():
                    pltpu.make_async_copy(
                        result.at[rows, :], target.at[:, columns], out_recv.at[index]
                    ).start()

    def dot(left, right):
        return jnp.dot(left, right, preferred_element_type=jnp.float32)

    def dot_nt(left, right):
        return lax.dot_general(
            left, right, (((1,), (1,)), ((), ())), preferred_element_type=jnp.float32
        )

    def flip(ref, target):
        for start in range(0, tokens, row_tokens):
            part = ref[start : start + row_tokens, :].astype(jnp.float32)
            target[:, start : start + row_tokens] = jnp.transpose(part).astype(target.dtype)

    groups = []
    for row in range(TILE_H):
        low, high = max(row - 1, 0), min(row + 1, TILE_H - 1)
        count = (high + 1 - low) * row_tokens
        for plane in range(2):
            groups.append(
                (
                    plane * plane_tokens + row * row_tokens,
                    [(0, low * row_tokens), (count, plane_tokens + low * row_tokens)],
                    count,
                )
            )

    def finish_keys(row):
        for plane in range(2):
            start = plane * plane_tokens + row * row_tokens
            span = slice(start, start + row_tokens)
            dv_all[span, :] = dv_sum[span, :].astype(jnp.bfloat16)
            dk_all[span, :] = (dk_sum[span, :] * scaling).astype(jnp.bfloat16)
        send_row(3, row)
        send_row(2, row)

    @pl.when(owns)
    def _():
        for block in range(devices):
            listed = slots_ref[block : block + 1, :]
            ids = lax.broadcasted_iota(jnp.int32, (devices, listed.shape[1]), 0)
            hit = jnp.where(ids == listed, 0.0, -1e30)
            best = jnp.max(hit, axis=1, keepdims=True)
            bias[:, block * BLOCK : (block + 1) * BLOCK] = jnp.broadcast_to(best, (devices, BLOCK))
        dk_sum[...] = jnp.zeros_like(dk_sum)
        dv_sum[...] = jnp.zeros_like(dv_sum)

        arrived(0)
        arrived(1)
        flip(k_all, kt_all)
        for index, (start, ranges, count) in enumerate(groups):
            queries = q_all[start : start + row_tokens, :]
            scores = []
            for offset, first in ranges:
                part = dot_nt(k_all[first : first + count, :], queries) * scaling
                blocks = count // BLOCK
                shift = bias[first // BLOCK : first // BLOCK + blocks, start : start + row_tokens]
                part = part.reshape(blocks, BLOCK, row_tokens) + shift[:, None, :]
                scores.append(part.reshape(count, row_tokens))
            peak = jnp.maximum(
                jnp.max(scores[0], axis=0, keepdims=True), jnp.max(scores[1], axis=0, keepdims=True)
            )
            powers = [jnp.exp(part - peak) for part in scores]
            total = jnp.sum(powers[0], axis=0, keepdims=True) + jnp.sum(
                powers[1], axis=0, keepdims=True
            )
            inverse = 1.0 / total
            for (offset, first), part in zip(ranges, powers):
                probs[index, offset : offset + count, :] = part * inverse

        arrived(2)
        flip(v_all, vt_all)
        for index, (start, ranges, count) in enumerate(groups):
            mixed = jnp.zeros((HEAD, row_tokens), jnp.float32)
            for offset, first in ranges:
                weights = probs[index, offset : offset + count, :].astype(jnp.bfloat16)
                mixed += dot(vt_all[:, first : first + count], weights)
            ot_all[:, start : start + row_tokens] = mixed.astype(jnp.bfloat16)
            o_all[start : start + row_tokens, :] = jnp.transpose(mixed).astype(jnp.bfloat16)
            if index % 2 == 1:
                send_row(0, index // 2)

        arrived(3)
        flip(g_all, gt_all)
        for index, (start, ranges, count) in enumerate(groups):
            span = slice(start, start + row_tokens)
            delta = jnp.sum(
                gt_all[:, span].astype(jnp.float32) * ot_all[:, span].astype(jnp.float32),
                axis=0,
                keepdims=True,
            )
            grads = g_all[span, :]
            queries = q_all[span, :]
            turned = jnp.zeros((HEAD, row_tokens), jnp.float32)
            for offset, first in ranges:
                keys = slice(first, first + count)
                exact = probs[index, offset : offset + count, :]
                dv_sum[keys, :] += dot(exact.astype(jnp.bfloat16), grads)
                product = dot_nt(v_all[keys, :], grads)
                slopes = (exact * (product - delta)).astype(jnp.bfloat16)
                turned += dot(kt_all[:, keys], slopes)
                dk_sum[keys, :] += dot(slopes, queries)
            dq_all[span, :] = jnp.transpose(turned * scaling).astype(jnp.bfloat16)
            if index % 2 == 1:
                row = index // 2
                send_row(1, row)
                if row >= 1:
                    finish_keys(row - 1)
        finish_keys(TILE_H - 1)

        for index in range(4):
            sent = sources[index].at[:, : (HEADS - 1) * HEAD]
            pltpu.make_async_copy(sent, sent, in_send.at[index]).wait()
            sent = results[index].at[: (devices - 1) * BLOCK, :]
            pltpu.make_async_copy(sent, sent, out_send.at[index]).wait()

    @pl.when(jnp.logical_not(owns))
    def _():
        for index in range(4):
            pltpu.make_async_copy(sources[index], sources[index], in_send.at[index]).wait()

    for index in range(4):
        pltpu.make_async_copy(targets[index], targets[index], out_recv.at[index]).wait()


def exchange_sizes(devices):
    tokens = devices * BLOCK
    row_tokens = tokens // (2 * TILE_H)
    return tokens, (2 * TILE_H, 6 * row_tokens, row_tokens)


def exchange_body(query, key_rows, value, grad_out, kv_slots):
    devices = lax.axis_size("ctx")
    tokens, probs_shape = exchange_sizes(devices)
    low = lambda *shape: pltpu.VMEM(shape, jnp.bfloat16)
    full = lambda *shape: pltpu.VMEM(shape, jnp.float32)
    anywhere = pl.BlockSpec(memory_space=pl.ANY)
    whole = jax.ShapeDtypeStruct(query.shape, query.dtype)
    return pl.pallas_call(
        functools.partial(exchange_kernel, devices),
        out_shape=(whole,) * 4,
        in_specs=[anywhere] * 4 + [pl.BlockSpec(memory_space=pltpu.VMEM)],
        out_specs=(anywhere,) * 4,
        scratch_shapes=[low(tokens, HEAD)] * 4
        + [low(HEAD, tokens)] * 4
        + [low(tokens, HEAD)] * 4
        + [full(tokens, HEAD)] * 2
        + [full(devices, tokens), full(*probs_shape)]
        + [pltpu.SemaphoreType.DMA((4,))] * 4,
        compiler_params=pltpu.CompilerParams(
            collective_id=0, has_side_effects=True, vmem_limit_bytes=VMEM_BYTES
        ),
    )(query, key_rows, value, grad_out, kv_slots)


def fits_exchange(devices, rows):
    if rows != devices * BLOCK or devices % (2 * TILE_H) or not devices // 2 <= HEADS <= devices:
        return False
    _, (groups, keys, queries) = exchange_sizes(devices)
    return groups * keys * queries * 4 <= VMEM_BYTES // 2


def solution(mesh):
    placed = P(("groups", "ctx"), None)

    def chosen(query, key_rows, value, grad_out, kv_slots):
        devices = mesh.shape["ctx"]
        rows = query.shape[0] // mesh.shape["groups"]
        return jax.shard_map(
            exchange_body if fits_exchange(devices, rows) else body,
            mesh=mesh,
            in_specs=(placed,) * 4 + (P(),),
            out_specs=(placed,) * 4,
            check_vma=False,
        )(query, key_rows, value, grad_out, kv_slots)

    return chosen
```

```python
import functools

import jax
import jax.numpy as jnp
from jax import lax
from jax.experimental import pallas as pl
from jax.experimental.pallas import tpu as pltpu
from jax.sharding import PartitionSpec as P

HEADS = 12
HEAD = 128
BLOCK = 128
TILE_H = 4


head_batch = 4
masked_score = -1e30
VMEM_BYTES = 63 * 1024 * 1024


def from_behind(value, axis, by):
    count = lax.axis_size(axis)
    return lax.ppermute(value, axis, [(i, (i + by) % count) for i in range(count)])


def neighbour_offsets(devices, blocks, tile_width):
    plane_size = TILE_H * tile_width
    total_slots = devices * blocks
    offset_set = set()
    for plane_step in (0, 1):
        for row_step in (-1, 0, 1):
            for col_step in (-1, 0, 1):
                offset = (plane_step * plane_size + row_step * tile_width + col_step) % total_slots
                target = offset % total_slots // blocks
                if target > devices // 2:
                    target = target - devices
                if target != 0:
                    offset_set.add(target)
    return offset_set


def split_heads(tensor):
    return tensor.reshape(
        tensor.shape[0], HEADS // head_batch, head_batch, tensor.shape[1] // HEADS
    )


def pick_group(tensor, group_index):
    return lax.dynamic_index_in_dim(tensor, group_index, 1, keepdims=False)


def join_heads(stacked):
    return jnp.moveaxis(stacked, 0, 1).reshape(stacked.shape[1], -1)


def apply_mask(scores, block_mask):
    heads_here, row_total, col_total = scores.shape
    row_blocks, col_blocks = block_mask.shape
    shaped = scores.reshape(
        heads_here, row_blocks, row_total // row_blocks, col_blocks, col_total // col_blocks
    )
    shaped = jnp.where(block_mask[None, :, None, :, None], shaped, masked_score)
    return shaped.reshape(heads_here, row_total, col_total)


def forward_group(group_index, queries, keys, values, allowed, scaling):
    query_part = pick_group(queries, group_index)
    key_part = pick_group(keys, group_index)
    value_part = pick_group(values, group_index)
    scores = (
        jnp.einsum("qhd,khd->hqk", query_part, key_part, preferred_element_type=jnp.float32)
        * scaling
    )
    scores = apply_mask(scores, allowed)
    peak_score = jnp.max(scores, axis=2, keepdims=True)
    denominator = jnp.sum(jnp.exp(scores - peak_score), axis=2, keepdims=True)
    log_norm = peak_score + jnp.log(denominator)
    weights = jnp.exp(scores - log_norm).astype(jnp.bfloat16)
    mixed_rows = jnp.einsum("hqk,khd->qhd", weights, value_part, preferred_element_type=jnp.float32)
    return (mixed_rows, log_norm[:, :, 0])


def query_group(
    group_index, queries, keys, values, gradients, log_split, delta_split, allowed, scaling
):
    query_part = pick_group(queries, group_index)
    key_part = pick_group(keys, group_index)
    value_part = pick_group(values, group_index)
    grad_part = pick_group(gradients, group_index)
    log_part = jnp.transpose(pick_group(log_split, group_index))
    delta_part = jnp.transpose(pick_group(delta_split, group_index))
    scores = (
        jnp.einsum("qhd,khd->hqk", query_part, key_part, preferred_element_type=jnp.float32)
        * scaling
    )
    scores = apply_mask(scores, allowed)
    weights = jnp.exp(scores - log_part[:, :, None])
    grad_probs = jnp.einsum(
        "qhd,khd->hqk", grad_part, value_part, preferred_element_type=jnp.float32
    )
    grad_scores = (weights * (grad_probs - delta_part[:, :, None])).astype(jnp.bfloat16)
    return (
        jnp.einsum("hqk,khd->qhd", grad_scores, key_part, preferred_element_type=jnp.float32)
        * scaling
    )


def key_group(
    group_index, keys, values, queries, gradients, log_split, delta_split, back_mask, scaling
):
    key_part = pick_group(keys, group_index)
    value_part = pick_group(values, group_index)
    query_part = pick_group(queries, group_index)
    grad_part = pick_group(gradients, group_index)
    log_part = jnp.transpose(pick_group(log_split, group_index))
    delta_part = jnp.transpose(pick_group(delta_split, group_index))
    scores = (
        jnp.einsum("khd,chd->hkc", key_part, query_part, preferred_element_type=jnp.float32)
        * scaling
    )
    scores = apply_mask(scores, back_mask)
    weights = jnp.exp(scores - log_part[:, None, :])
    grad_probs = jnp.einsum(
        "khd,chd->hkc", value_part, grad_part, preferred_element_type=jnp.float32
    )
    grad_scores = (weights * (grad_probs - delta_part[:, None, :])).astype(jnp.bfloat16)
    grad_values = jnp.einsum(
        "hkc,chd->khd", weights.astype(jnp.bfloat16), grad_part, preferred_element_type=jnp.float32
    )
    grad_keys = (
        jnp.einsum("hkc,chd->khd", grad_scores, query_part, preferred_element_type=jnp.float32)
        * scaling
    )
    return (grad_keys, grad_values)


def body(query, key_rows, value, grad_out, kv_slots):
    devices = lax.axis_size("ctx")
    device_index = lax.axis_index("ctx")
    row_count = query.shape[0]
    blocks = row_count // BLOCK
    tile_width = devices * blocks // (2 * TILE_H)
    offset_set = neighbour_offsets(devices, blocks, tile_width)
    visit_order = sorted(offset_set)
    distances = [0] + visit_order
    local_slots = jnp.arange(blocks, dtype=jnp.int32)
    cand_slots = jnp.concatenate(
        [(device_index + distance) % devices * blocks + local_slots for distance in distances]
    ).astype(jnp.int32)
    own_blocks = device_index * blocks + local_slots
    own_lists = lax.dynamic_slice_in_dim(kv_slots, device_index * blocks, blocks, 0)
    allowed = jnp.any(own_lists[:, :, None] == cand_slots[None, None, :], axis=1)
    cand_lists = jnp.take(kv_slots, cand_slots, axis=0)
    back_mask = jnp.any(cand_lists[None, :, :] == own_blocks[:, None, None], axis=2)
    scaling = HEAD ** (-0.5)
    groups = HEADS // head_batch
    group_ids = jnp.arange(groups)
    arrived = [from_behind((key_rows, value), "ctx", -distance) for distance in visit_order]
    cand_keys = split_heads(jnp.concatenate([key_rows] + [item[0] for item in arrived], axis=0))
    cand_values = split_heads(jnp.concatenate([value] + [item[1] for item in arrived], axis=0))
    queries = split_heads(query)
    mixed_all, norm_all = lax.map(
        lambda group_index: forward_group(
            group_index, queries, cand_keys, cand_values, allowed, scaling
        ),
        group_ids,
    )
    out = join_heads(mixed_all).astype(jnp.bfloat16)
    log_rows = jnp.transpose(norm_all.reshape(HEADS, row_count))
    delta_rows = jnp.sum(
        (grad_out.astype(jnp.float32) * out.astype(jnp.float32)).reshape(row_count, HEADS, -1),
        axis=2,
    )
    gradients = split_heads(grad_out)
    log_split = log_rows.reshape(row_count, groups, head_batch)
    delta_split = delta_rows.reshape(row_count, groups, head_batch)
    query_terms = lax.map(
        lambda group_index: query_group(
            group_index,
            queries,
            cand_keys,
            cand_values,
            gradients,
            log_split,
            delta_split,
            allowed,
            scaling,
        ),
        group_ids,
    )
    grad_query = join_heads(query_terms).astype(jnp.bfloat16)
    returned = [from_behind((query, grad_out), "ctx", -distance) for distance in visit_order]
    cand_queries = jnp.concatenate([query] + [item[0] for item in returned], axis=0)
    cand_grads = jnp.concatenate([grad_out] + [item[1] for item in returned], axis=0)
    row_terms = [from_behind((log_rows, delta_rows), "ctx", -distance) for distance in visit_order]
    cand_log = jnp.concatenate([log_rows] + [item[0] for item in row_terms], axis=0).reshape(
        -1, groups, head_batch
    )
    cand_delta = jnp.concatenate([delta_rows] + [item[1] for item in row_terms], axis=0).reshape(
        -1, groups, head_batch
    )
    own_keys = split_heads(key_rows)
    own_values = split_heads(value)
    split_queries = split_heads(cand_queries)
    split_grads = split_heads(cand_grads)
    key_terms, value_terms = lax.map(
        lambda group_index: key_group(
            group_index,
            own_keys,
            own_values,
            split_queries,
            split_grads,
            cand_log,
            cand_delta,
            back_mask,
            scaling,
        ),
        group_ids,
    )
    grad_key = join_heads(key_terms).astype(jnp.bfloat16)
    grad_value = join_heads(value_terms).astype(jnp.bfloat16)
    return (out, grad_query, grad_key, grad_value)


def head_owner(head, devices):
    chips = devices // 2
    first = (chips - (HEADS - chips)) // 2
    return jnp.where(head < chips, 2 * head, 2 * (head - chips + first) + 1)


def head_of(device, devices):
    chips = devices // 2
    extra = HEADS - chips
    first = (chips - extra) // 2
    chip = device // 2
    odd = device % 2
    inside = (chip >= first) & (chip < first + extra)
    second = jnp.where(inside, chips + chip - first, -1)
    return jnp.where(odd == 0, jnp.where(chip < HEADS, chip, -1), second)


def exchange_kernel(
    devices,
    query_ref,
    key_ref,
    value_ref,
    grad_ref,
    slots_ref,
    out_ref,
    dq_ref,
    dk_ref,
    dv_ref,
    q_all,
    k_all,
    v_all,
    g_all,
    kt_all,
    vt_all,
    gt_all,
    ot_all,
    o_all,
    dq_all,
    dk_all,
    dv_all,
    dk_sum,
    dv_sum,
    bias,
    probs,
    in_send,
    in_recv,
    out_send,
    out_recv,
):
    me = lax.axis_index("ctx")
    my_head = head_of(me, devices)
    owns = my_head >= 0
    tokens = devices * BLOCK
    width = devices // (2 * TILE_H)
    row_tokens = width * BLOCK
    plane_tokens = tokens // 2
    scaling = HEAD ** (-0.5)

    barrier = pltpu.get_barrier_semaphore()
    for step in range(1, devices):
        pl.semaphore_signal(
            barrier,
            inc=1,
            device_id={"ctx": lax.rem(me + step, devices)},
            device_id_type=pl.DeviceIdType.MESH,
        )
    pl.semaphore_wait(barrier, devices - 1)

    sources = (key_ref, query_ref, value_ref, grad_ref)
    landings = (k_all, q_all, v_all, g_all)
    own_rows = pl.ds(pl.multiple_of(me * BLOCK, BLOCK), BLOCK)

    half = me // (devices // 2)
    chips = devices // 2
    pairs = HEADS // 2

    def send_inputs(index):
        source, landing = sources[index], landings[index]

        def one(step, carry):
            place = lax.rem(me + step, pairs)
            for side in (1 - half, half):
                head = jnp.where(
                    place < chips // 2,
                    place + side * (chips // 2),
                    chips + place - chips // 2 + side * ((HEADS - chips) // 2),
                )
                owner = head_owner(head, devices)
                columns = pl.ds(pl.multiple_of(head * HEAD, HEAD), HEAD)

                @pl.when(owner != me)
                def _():
                    pltpu.make_async_remote_copy(
                        src_ref=source.at[:, columns],
                        dst_ref=landing.at[own_rows, :],
                        send_sem=in_send.at[index],
                        recv_sem=in_recv.at[index],
                        device_id={"ctx": owner},
                        device_id_type=pl.DeviceIdType.MESH,
                    ).start()

                @pl.when(owner == me)
                def _():
                    pltpu.make_async_copy(
                        source.at[:, columns], landing.at[own_rows, :], in_recv.at[index]
                    ).start()

            return carry

        lax.fori_loop(0, pairs, one, 0)

    def inputs_sent(index):
        @pl.when(owns)
        def _():
            sent = sources[index].at[:, : (HEADS - 1) * HEAD]
            pltpu.make_async_copy(sent, sent, in_send.at[index]).wait()

        @pl.when(jnp.logical_not(owns))
        def _():
            pltpu.make_async_copy(sources[index], sources[index], in_send.at[index]).wait()

    send_inputs(0)
    send_inputs(1)
    inputs_sent(0)
    send_inputs(2)
    inputs_sent(1)
    send_inputs(3)

    def arrived(index):
        pltpu.make_async_copy(landings[index], landings[index], in_recv.at[index]).wait()

    results = (o_all, dq_all, dk_all, dv_all)
    targets = (out_ref, dq_ref, dk_ref, dv_ref)

    def send_row(index, row):
        result, target = results[index], targets[index]
        columns = pl.ds(pl.multiple_of(my_head * HEAD, HEAD), HEAD)
        for column in range(width):
            for side in (1 - half, half):
                other = side * (devices // 2) + row * width + column
                rows = pl.ds(pl.multiple_of(other * BLOCK, BLOCK), BLOCK)

                @pl.when(other != me)
                def _():
                    pltpu.make_async_remote_copy(
                        src_ref=result.at[rows, :],
                        dst_ref=target.at[:, columns],
                        send_sem=out_send.at[index],
                        recv_sem=out_recv.at[index],
                        device_id={"ctx": other},
                        device_id_type=pl.DeviceIdType.MESH,
                    ).start()

                @pl.when(other == me)
                def _():
                    pltpu.make_async_copy(
                        result.at[rows, :], target.at[:, columns], out_recv.at[index]
                    ).start()

    def dot(left, right):
        return jnp.dot(left, right, preferred_element_type=jnp.float32)

    def dot_nt(left, right):
        return lax.dot_general(
            left, right, (((1,), (1,)), ((), ())), preferred_element_type=jnp.float32
        )

    def flip(ref, target):
        for start in range(0, tokens, row_tokens):
            part = ref[start : start + row_tokens, :].astype(jnp.float32)
            target[:, start : start + row_tokens] = jnp.transpose(part).astype(target.dtype)

    groups = []
    for row in range(TILE_H):
        low, high = max(row - 1, 0), min(row + 1, TILE_H - 1)
        count = (high + 1 - low) * row_tokens
        for plane in range(2):
            groups.append(
                (
                    plane * plane_tokens + row * row_tokens,
                    [(0, low * row_tokens), (count, plane_tokens + low * row_tokens)],
                    count,
                )
            )

    def finish_keys(row):
        for plane in range(2):
            start = plane * plane_tokens + row * row_tokens
            span = slice(start, start + row_tokens)
            dv_all[span, :] = dv_sum[span, :].astype(jnp.bfloat16)
            dk_all[span, :] = (dk_sum[span, :] * scaling).astype(jnp.bfloat16)
        send_row(3, row)
        send_row(2, row)

    @pl.when(owns)
    def _():
        for block in range(devices):
            listed = slots_ref[block : block + 1, :]
            ids = lax.broadcasted_iota(jnp.int32, (devices, listed.shape[1]), 0)
            hit = jnp.where(ids == listed, 0.0, -1e30)
            best = jnp.max(hit, axis=1, keepdims=True)
            bias[:, block * BLOCK : (block + 1) * BLOCK] = jnp.broadcast_to(best, (devices, BLOCK))
        dk_sum[...] = jnp.zeros_like(dk_sum)
        dv_sum[...] = jnp.zeros_like(dv_sum)

        arrived(0)
        arrived(1)
        flip(k_all, kt_all)
        for index, (start, ranges, count) in enumerate(groups):
            queries = q_all[start : start + row_tokens, :]
            scores = []
            for offset, first in ranges:
                part = dot_nt(k_all[first : first + count, :], queries) * scaling
                blocks = count // BLOCK
                shift = bias[first // BLOCK : first // BLOCK + blocks, start : start + row_tokens]
                part = part.reshape(blocks, BLOCK, row_tokens) + shift[:, None, :]
                scores.append(part.reshape(count, row_tokens))
            peak = jnp.maximum(
                jnp.max(scores[0], axis=0, keepdims=True), jnp.max(scores[1], axis=0, keepdims=True)
            )
            powers = [jnp.exp(part - peak) for part in scores]
            total = jnp.sum(powers[0], axis=0, keepdims=True) + jnp.sum(
                powers[1], axis=0, keepdims=True
            )
            inverse = 1.0 / total
            for (offset, first), part in zip(ranges, powers):
                probs[index, offset : offset + count, :] = part * inverse

        arrived(2)
        flip(v_all, vt_all)
        for index, (start, ranges, count) in enumerate(groups):
            mixed = jnp.zeros((HEAD, row_tokens), jnp.float32)
            for offset, first in ranges:
                weights = probs[index, offset : offset + count, :].astype(jnp.bfloat16)
                mixed += dot(vt_all[:, first : first + count], weights)
            ot_all[:, start : start + row_tokens] = mixed.astype(jnp.bfloat16)
            o_all[start : start + row_tokens, :] = jnp.transpose(mixed).astype(jnp.bfloat16)
            if index % 2 == 1:
                send_row(0, index // 2)

        arrived(3)
        flip(g_all, gt_all)
        for index, (start, ranges, count) in enumerate(groups):
            span = slice(start, start + row_tokens)
            delta = jnp.sum(
                gt_all[:, span].astype(jnp.float32) * ot_all[:, span].astype(jnp.float32),
                axis=0,
                keepdims=True,
            )
            grads = g_all[span, :]
            queries = q_all[span, :]
            turned = jnp.zeros((HEAD, row_tokens), jnp.float32)
            for offset, first in ranges:
                keys = slice(first, first + count)
                exact = probs[index, offset : offset + count, :]
                dv_sum[keys, :] += dot(exact.astype(jnp.bfloat16), grads)
                product = dot_nt(v_all[keys, :], grads)
                slopes = (exact * (product - delta)).astype(jnp.bfloat16)
                turned += dot(kt_all[:, keys], slopes)
                dk_sum[keys, :] += dot(slopes, queries)
            dq_all[span, :] = jnp.transpose(turned * scaling).astype(jnp.bfloat16)
            if index % 2 == 1:
                row = index // 2
                send_row(1, row)
                if row >= 1:
                    finish_keys(row - 1)
        finish_keys(TILE_H - 1)

        for index in range(4):
            sent = results[index].at[: (devices - 1) * BLOCK, :]
            pltpu.make_async_copy(sent, sent, out_send.at[index]).wait()

    inputs_sent(2)
    inputs_sent(3)
    for index in range(4):
        pltpu.make_async_copy(targets[index], targets[index], out_recv.at[index]).wait()


def copy_kernel(*refs):
    sources, targets, sems = refs[:4], refs[4:8], refs[8]
    copies = [
        pltpu.make_async_copy(source, target, sems.at[index])
        for index, (source, target) in enumerate(zip(sources, targets))
    ]
    for copy in copies:
        copy.start()
    for copy in copies:
        copy.wait()


def exchange_sizes(devices):
    tokens = devices * BLOCK
    row_tokens = tokens // (2 * TILE_H)
    return tokens, (2 * TILE_H, 6 * row_tokens, row_tokens)


def exchange_body(query, key_rows, value, grad_out, kv_slots):
    devices = lax.axis_size("ctx")
    tokens, probs_shape = exchange_sizes(devices)
    low = lambda *shape: pltpu.VMEM(shape, jnp.bfloat16)
    full = lambda *shape: pltpu.VMEM(shape, jnp.float32)
    anywhere = pl.BlockSpec(memory_space=pl.ANY)
    whole = jax.ShapeDtypeStruct(query.shape, query.dtype)
    landed = pl.pallas_call(
        functools.partial(exchange_kernel, devices),
        out_shape=(whole,) * 4,
        in_specs=[anywhere] * 4 + [pl.BlockSpec(memory_space=pltpu.VMEM)],
        out_specs=(anywhere,) * 4,
        scratch_shapes=[low(tokens, HEAD)] * 4
        + [low(HEAD, tokens)] * 4
        + [low(tokens, HEAD)] * 4
        + [full(tokens, HEAD)] * 2
        + [full(devices, tokens), full(*probs_shape)]
        + [pltpu.SemaphoreType.DMA((4,))] * 4,
        compiler_params=pltpu.CompilerParams(
            collective_id=0, has_side_effects=True, vmem_limit_bytes=VMEM_BYTES
        ),
    )(query, key_rows, value, grad_out, kv_slots)
    return pl.pallas_call(
        copy_kernel,
        out_shape=(whole,) * 4,
        in_specs=[anywhere] * 4,
        out_specs=(anywhere,) * 4,
        scratch_shapes=[pltpu.SemaphoreType.DMA((4,))],
        compiler_params=pltpu.CompilerParams(vmem_limit_bytes=VMEM_BYTES),
    )(*landed)


def fits_exchange(devices, rows):
    if rows != devices * BLOCK or devices % (2 * TILE_H) or not devices // 2 <= HEADS <= devices:
        return False
    _, (groups, keys, queries) = exchange_sizes(devices)
    return groups * keys * queries * 4 <= VMEM_BYTES // 2


def solution(mesh):
    placed = P(("groups", "ctx"), None)

    def chosen(query, key_rows, value, grad_out, kv_slots):
        devices = mesh.shape["ctx"]
        rows = query.shape[0] // mesh.shape["groups"]
        return jax.shard_map(
            exchange_body if fits_exchange(devices, rows) else body,
            mesh=mesh,
            in_specs=(placed,) * 4 + (P(),),
            out_specs=(placed,) * 4,
            check_vma=False,
        )(query, key_rows, value, grad_out, kv_slots)

    return chosen
```

```python
import functools

import jax
import jax.numpy as jnp
from jax import lax
from jax.experimental import pallas as pl
from jax.experimental.pallas import tpu as pltpu
from jax.sharding import PartitionSpec as P

HEADS = 12
HEAD = 128
BLOCK = 128
TILE_H = 4


head_batch = 4
masked_score = -1e30
VMEM_BYTES = 63 * 1024 * 1024


def from_behind(value, axis, by):
    count = lax.axis_size(axis)
    return lax.ppermute(value, axis, [(i, (i + by) % count) for i in range(count)])


def neighbour_offsets(devices, blocks, tile_width):
    plane_size = TILE_H * tile_width
    total_slots = devices * blocks
    offset_set = set()
    for plane_step in (0, 1):
        for row_step in (-1, 0, 1):
            for col_step in (-1, 0, 1):
                offset = (plane_step * plane_size + row_step * tile_width + col_step) % total_slots
                target = offset % total_slots // blocks
                if target > devices // 2:
                    target = target - devices
                if target != 0:
                    offset_set.add(target)
    return offset_set


def split_heads(tensor):
    return tensor.reshape(
        tensor.shape[0], HEADS // head_batch, head_batch, tensor.shape[1] // HEADS
    )


def pick_group(tensor, group_index):
    return lax.dynamic_index_in_dim(tensor, group_index, 1, keepdims=False)


def join_heads(stacked):
    return jnp.moveaxis(stacked, 0, 1).reshape(stacked.shape[1], -1)


def apply_mask(scores, block_mask):
    heads_here, row_total, col_total = scores.shape
    row_blocks, col_blocks = block_mask.shape
    shaped = scores.reshape(
        heads_here, row_blocks, row_total // row_blocks, col_blocks, col_total // col_blocks
    )
    shaped = jnp.where(block_mask[None, :, None, :, None], shaped, masked_score)
    return shaped.reshape(heads_here, row_total, col_total)


def forward_group(group_index, queries, keys, values, allowed, scaling):
    query_part = pick_group(queries, group_index)
    key_part = pick_group(keys, group_index)
    value_part = pick_group(values, group_index)
    scores = (
        jnp.einsum("qhd,khd->hqk", query_part, key_part, preferred_element_type=jnp.float32)
        * scaling
    )
    scores = apply_mask(scores, allowed)
    peak_score = jnp.max(scores, axis=2, keepdims=True)
    denominator = jnp.sum(jnp.exp(scores - peak_score), axis=2, keepdims=True)
    log_norm = peak_score + jnp.log(denominator)
    weights = jnp.exp(scores - log_norm).astype(jnp.bfloat16)
    mixed_rows = jnp.einsum("hqk,khd->qhd", weights, value_part, preferred_element_type=jnp.float32)
    return (mixed_rows, log_norm[:, :, 0])


def query_group(
    group_index, queries, keys, values, gradients, log_split, delta_split, allowed, scaling
):
    query_part = pick_group(queries, group_index)
    key_part = pick_group(keys, group_index)
    value_part = pick_group(values, group_index)
    grad_part = pick_group(gradients, group_index)
    log_part = jnp.transpose(pick_group(log_split, group_index))
    delta_part = jnp.transpose(pick_group(delta_split, group_index))
    scores = (
        jnp.einsum("qhd,khd->hqk", query_part, key_part, preferred_element_type=jnp.float32)
        * scaling
    )
    scores = apply_mask(scores, allowed)
    weights = jnp.exp(scores - log_part[:, :, None])
    grad_probs = jnp.einsum(
        "qhd,khd->hqk", grad_part, value_part, preferred_element_type=jnp.float32
    )
    grad_scores = (weights * (grad_probs - delta_part[:, :, None])).astype(jnp.bfloat16)
    return (
        jnp.einsum("hqk,khd->qhd", grad_scores, key_part, preferred_element_type=jnp.float32)
        * scaling
    )


def key_group(
    group_index, keys, values, queries, gradients, log_split, delta_split, back_mask, scaling
):
    key_part = pick_group(keys, group_index)
    value_part = pick_group(values, group_index)
    query_part = pick_group(queries, group_index)
    grad_part = pick_group(gradients, group_index)
    log_part = jnp.transpose(pick_group(log_split, group_index))
    delta_part = jnp.transpose(pick_group(delta_split, group_index))
    scores = (
        jnp.einsum("khd,chd->hkc", key_part, query_part, preferred_element_type=jnp.float32)
        * scaling
    )
    scores = apply_mask(scores, back_mask)
    weights = jnp.exp(scores - log_part[:, None, :])
    grad_probs = jnp.einsum(
        "khd,chd->hkc", value_part, grad_part, preferred_element_type=jnp.float32
    )
    grad_scores = (weights * (grad_probs - delta_part[:, None, :])).astype(jnp.bfloat16)
    grad_values = jnp.einsum(
        "hkc,chd->khd", weights.astype(jnp.bfloat16), grad_part, preferred_element_type=jnp.float32
    )
    grad_keys = (
        jnp.einsum("hkc,chd->khd", grad_scores, query_part, preferred_element_type=jnp.float32)
        * scaling
    )
    return (grad_keys, grad_values)


def body(query, key_rows, value, grad_out, kv_slots):
    devices = lax.axis_size("ctx")
    device_index = lax.axis_index("ctx")
    row_count = query.shape[0]
    blocks = row_count // BLOCK
    tile_width = devices * blocks // (2 * TILE_H)
    offset_set = neighbour_offsets(devices, blocks, tile_width)
    visit_order = sorted(offset_set)
    distances = [0] + visit_order
    local_slots = jnp.arange(blocks, dtype=jnp.int32)
    cand_slots = jnp.concatenate(
        [(device_index + distance) % devices * blocks + local_slots for distance in distances]
    ).astype(jnp.int32)
    own_blocks = device_index * blocks + local_slots
    own_lists = lax.dynamic_slice_in_dim(kv_slots, device_index * blocks, blocks, 0)
    allowed = jnp.any(own_lists[:, :, None] == cand_slots[None, None, :], axis=1)
    cand_lists = jnp.take(kv_slots, cand_slots, axis=0)
    back_mask = jnp.any(cand_lists[None, :, :] == own_blocks[:, None, None], axis=2)
    scaling = HEAD ** (-0.5)
    groups = HEADS // head_batch
    group_ids = jnp.arange(groups)
    arrived = [from_behind((key_rows, value), "ctx", -distance) for distance in visit_order]
    cand_keys = split_heads(jnp.concatenate([key_rows] + [item[0] for item in arrived], axis=0))
    cand_values = split_heads(jnp.concatenate([value] + [item[1] for item in arrived], axis=0))
    queries = split_heads(query)
    mixed_all, norm_all = lax.map(
        lambda group_index: forward_group(
            group_index, queries, cand_keys, cand_values, allowed, scaling
        ),
        group_ids,
    )
    out = join_heads(mixed_all).astype(jnp.bfloat16)
    log_rows = jnp.transpose(norm_all.reshape(HEADS, row_count))
    delta_rows = jnp.sum(
        (grad_out.astype(jnp.float32) * out.astype(jnp.float32)).reshape(row_count, HEADS, -1),
        axis=2,
    )
    gradients = split_heads(grad_out)
    log_split = log_rows.reshape(row_count, groups, head_batch)
    delta_split = delta_rows.reshape(row_count, groups, head_batch)
    query_terms = lax.map(
        lambda group_index: query_group(
            group_index,
            queries,
            cand_keys,
            cand_values,
            gradients,
            log_split,
            delta_split,
            allowed,
            scaling,
        ),
        group_ids,
    )
    grad_query = join_heads(query_terms).astype(jnp.bfloat16)
    returned = [from_behind((query, grad_out), "ctx", -distance) for distance in visit_order]
    cand_queries = jnp.concatenate([query] + [item[0] for item in returned], axis=0)
    cand_grads = jnp.concatenate([grad_out] + [item[1] for item in returned], axis=0)
    row_terms = [from_behind((log_rows, delta_rows), "ctx", -distance) for distance in visit_order]
    cand_log = jnp.concatenate([log_rows] + [item[0] for item in row_terms], axis=0).reshape(
        -1, groups, head_batch
    )
    cand_delta = jnp.concatenate([delta_rows] + [item[1] for item in row_terms], axis=0).reshape(
        -1, groups, head_batch
    )
    own_keys = split_heads(key_rows)
    own_values = split_heads(value)
    split_queries = split_heads(cand_queries)
    split_grads = split_heads(cand_grads)
    key_terms, value_terms = lax.map(
        lambda group_index: key_group(
            group_index,
            own_keys,
            own_values,
            split_queries,
            split_grads,
            cand_log,
            cand_delta,
            back_mask,
            scaling,
        ),
        group_ids,
    )
    grad_key = join_heads(key_terms).astype(jnp.bfloat16)
    grad_value = join_heads(value_terms).astype(jnp.bfloat16)
    return (out, grad_query, grad_key, grad_value)


def head_owner(head, devices):
    chips = devices // 2
    first = (chips - (HEADS - chips)) // 2
    return jnp.where(head < chips, 2 * head, 2 * (head - chips + first) + 1)


def head_of(device, devices):
    chips = devices // 2
    extra = HEADS - chips
    first = (chips - extra) // 2
    chip = device // 2
    odd = device % 2
    inside = (chip >= first) & (chip < first + extra)
    second = jnp.where(inside, chips + chip - first, -1)
    return jnp.where(odd == 0, jnp.where(chip < HEADS, chip, -1), second)


def exchange_kernel(
    devices,
    query_ref,
    key_ref,
    value_ref,
    grad_ref,
    slots_ref,
    out_ref,
    dq_ref,
    dk_ref,
    dv_ref,
    q_all,
    k_all,
    v_all,
    g_all,
    kt_all,
    vt_all,
    gt_all,
    ot_all,
    o_all,
    dq_all,
    dk_all,
    dv_all,
    dk_sum,
    dv_sum,
    bias,
    probs,
    staged,
    stage_sem,
    in_send,
    in_recv,
    out_send,
    out_recv,
):
    me = lax.axis_index("ctx")
    my_head = head_of(me, devices)
    owns = my_head >= 0
    tokens = devices * BLOCK
    width = devices // (2 * TILE_H)
    row_tokens = width * BLOCK
    plane_tokens = tokens // 2
    scaling = HEAD ** (-0.5)

    sources = (key_ref, query_ref, value_ref, grad_ref)
    landings = (k_all, q_all, v_all, g_all)
    own_rows = pl.ds(pl.multiple_of(me * BLOCK, BLOCK), BLOCK)
    barrier = pltpu.get_barrier_semaphore()
    for step in range(1, devices):
        pl.semaphore_signal(
            barrier,
            inc=1,
            device_id={"ctx": lax.rem(me + step, devices)},
            device_id_type=pl.DeviceIdType.MESH,
        )
    for index in range(4):
        for head in range(HEADS):
            pltpu.make_async_copy(
                sources[index].at[:, head * HEAD : (head + 1) * HEAD],
                staged.at[index, head],
                stage_sem.at[index],
            ).start()

    pl.semaphore_wait(barrier, devices - 1)

    half = me // (devices // 2)
    chips = devices // 2
    pairs = HEADS // 2

    def send_inputs(index):
        source, landing = sources[index], landings[index]
        pltpu.make_async_copy(staged.at[index], staged.at[index], stage_sem.at[index]).wait()

        def one(step, carry):
            place = lax.rem(me + step, pairs)
            for side in (1 - half, half):
                head = jnp.where(
                    place < chips // 2,
                    place + side * (chips // 2),
                    chips + place - chips // 2 + side * ((HEADS - chips) // 2),
                )
                owner = head_owner(head, devices)
                columns = pl.ds(pl.multiple_of(head * HEAD, HEAD), HEAD)

                @pl.when(owner != me)
                def _():
                    pltpu.make_async_remote_copy(
                        src_ref=staged.at[index, head],
                        dst_ref=landing.at[own_rows, :],
                        send_sem=in_send.at[index],
                        recv_sem=in_recv.at[index],
                        device_id={"ctx": owner},
                        device_id_type=pl.DeviceIdType.MESH,
                    ).start()

                @pl.when(owner == me)
                def _():
                    pltpu.make_async_copy(
                        source.at[:, columns], landing.at[own_rows, :], in_recv.at[index]
                    ).start()

            return carry

        lax.fori_loop(0, pairs, one, 0)

    for index in range(4):
        send_inputs(index)

    def arrived(index):
        pltpu.make_async_copy(landings[index], landings[index], in_recv.at[index]).wait()

    results = (o_all, dq_all, dk_all, dv_all)
    targets = (out_ref, dq_ref, dk_ref, dv_ref)

    def send_rows(indices, rows_here):
        for index in indices:
            result, target = results[index], targets[index]
            for column in range(width):
                for side in (1 - half, half):
                    for row in rows_here:
                        other = side * (devices // 2) + row * width + column
                        rows = pl.ds(pl.multiple_of(other * BLOCK, BLOCK), BLOCK)

                        @pl.when(other != me)
                        def _():
                            pltpu.make_async_remote_copy(
                                src_ref=result.at[rows, :],
                                dst_ref=target.at[my_head],
                                send_sem=out_send.at[index],
                                recv_sem=out_recv.at[index],
                                device_id={"ctx": other},
                                device_id_type=pl.DeviceIdType.MESH,
                            ).start()

                        @pl.when(other == me)
                        def _():
                            pltpu.make_async_copy(
                                result.at[rows, :], target.at[my_head], out_recv.at[index]
                            ).start()

    def dot(left, right):
        return jnp.dot(left, right, preferred_element_type=jnp.float32)

    def dot_nt(left, right):
        return lax.dot_general(
            left, right, (((1,), (1,)), ((), ())), preferred_element_type=jnp.float32
        )

    def flip(ref, target):
        for start in range(0, tokens, row_tokens):
            part = ref[start : start + row_tokens, :].astype(jnp.float32)
            target[:, start : start + row_tokens] = jnp.transpose(part).astype(target.dtype)

    groups = []
    for row in range(TILE_H):
        low, high = max(row - 1, 0), min(row + 1, TILE_H - 1)
        count = (high + 1 - low) * row_tokens
        for plane in range(2):
            groups.append(
                (
                    plane * plane_tokens + row * row_tokens,
                    [(0, low * row_tokens), (count, plane_tokens + low * row_tokens)],
                    count,
                )
            )

    def finish_keys(rows_here):
        for plane in range(2):
            start = plane * plane_tokens + rows_here[0] * row_tokens
            span = slice(start, start + len(rows_here) * row_tokens)
            dv_all[span, :] = dv_sum[span, :].astype(jnp.bfloat16)
            dk_all[span, :] = (dk_sum[span, :] * scaling).astype(jnp.bfloat16)
        send_rows((3, 2), rows_here)

    @pl.when(owns)
    def _():
        for block in range(devices):
            listed = slots_ref[block : block + 1, :]
            ids = lax.broadcasted_iota(jnp.int32, (devices, listed.shape[1]), 0)
            hit = jnp.where(ids == listed, 0.0, -1e30)
            best = jnp.max(hit, axis=1, keepdims=True)
            bias[:, block * BLOCK : (block + 1) * BLOCK] = jnp.broadcast_to(best, (devices, BLOCK))
        dk_sum[...] = jnp.zeros_like(dk_sum)
        dv_sum[...] = jnp.zeros_like(dv_sum)

        arrived(0)
        arrived(1)
        flip(k_all, kt_all)
        for index, (start, ranges, count) in enumerate(groups):
            queries = q_all[start : start + row_tokens, :]
            scores = []
            for offset, first in ranges:
                part = dot_nt(k_all[first : first + count, :], queries) * scaling
                blocks = count // BLOCK
                shift = bias[first // BLOCK : first // BLOCK + blocks, start : start + row_tokens]
                part = part.reshape(blocks, BLOCK, row_tokens) + shift[:, None, :]
                scores.append(part.reshape(count, row_tokens))
            peak = jnp.maximum(
                jnp.max(scores[0], axis=0, keepdims=True), jnp.max(scores[1], axis=0, keepdims=True)
            )
            powers = [jnp.exp(part - peak) for part in scores]
            total = jnp.sum(powers[0], axis=0, keepdims=True) + jnp.sum(
                powers[1], axis=0, keepdims=True
            )
            inverse = 1.0 / total
            for (offset, first), part in zip(ranges, powers):
                probs[index, offset : offset + count, :] = part * inverse

        arrived(2)
        flip(v_all, vt_all)
        for index, (start, ranges, count) in enumerate(groups):
            mixed = jnp.zeros((HEAD, row_tokens), jnp.float32)
            for offset, first in ranges:
                weights = probs[index, offset : offset + count, :].astype(jnp.bfloat16)
                mixed += dot(vt_all[:, first : first + count], weights)
            ot_all[:, start : start + row_tokens] = mixed.astype(jnp.bfloat16)
            o_all[start : start + row_tokens, :] = jnp.transpose(mixed).astype(jnp.bfloat16)
            if index % 4 == 3:
                send_rows((0,), (index // 2 - 1, index // 2))

        arrived(3)
        flip(g_all, gt_all)
        for index, (start, ranges, count) in enumerate(groups):
            span = slice(start, start + row_tokens)
            delta = jnp.sum(
                gt_all[:, span].astype(jnp.float32) * ot_all[:, span].astype(jnp.float32),
                axis=0,
                keepdims=True,
            )
            grads = g_all[span, :]
            queries = q_all[span, :]
            turned = jnp.zeros((HEAD, row_tokens), jnp.float32)
            for offset, first in ranges:
                keys = slice(first, first + count)
                exact = probs[index, offset : offset + count, :]
                dv_sum[keys, :] += dot(exact.astype(jnp.bfloat16), grads)
                product = dot_nt(v_all[keys, :], grads)
                slopes = (exact * (product - delta)).astype(jnp.bfloat16)
                turned += dot(kt_all[:, keys], slopes)
                dk_sum[keys, :] += dot(slopes, queries)
            dq_all[span, :] = jnp.transpose(turned * scaling).astype(jnp.bfloat16)
            if index % 4 == 3:
                send_rows((1,), (index // 2 - 1, index // 2))
            if index % 4 == 1 and index > 1:
                finish_keys((index // 2 - 2, index // 2 - 1))
        finish_keys((TILE_H - 2, TILE_H - 1))

        for index in range(4):
            sent = staged.at[index, pl.ds(0, HEADS - 1)]
            pltpu.make_async_copy(sent, sent, in_send.at[index]).wait()
            sent = results[index].at[: (devices - 1) * BLOCK, :]
            pltpu.make_async_copy(sent, sent, out_send.at[index]).wait()

    @pl.when(jnp.logical_not(owns))
    def _():
        for index in range(4):
            pltpu.make_async_copy(staged.at[index], staged.at[index], in_send.at[index]).wait()

    for index in range(4):
        pltpu.make_async_copy(targets[index], targets[index], out_recv.at[index]).wait()


def place_kernel(*refs):
    sources, targets, held, in_sem, out_sem = refs[:4], refs[4:8], refs[8], refs[9], refs[10]
    loads = [
        pltpu.make_async_copy(sources[index], held.at[index], in_sem.at[index])
        for index in range(4)
    ]
    for load in loads:
        load.start()
    for index, load in enumerate(loads):
        load.wait()
        for head in range(HEADS):
            pltpu.make_async_copy(
                held.at[index, head],
                targets[index].at[:, head * HEAD : (head + 1) * HEAD],
                out_sem.at[index],
            ).start()
    for index in range(4):
        pltpu.make_async_copy(held.at[index], held.at[index], out_sem.at[index]).wait()


def exchange_sizes(devices):
    tokens = devices * BLOCK
    row_tokens = tokens // (2 * TILE_H)
    return tokens, (2 * TILE_H, 6 * row_tokens, row_tokens)


def exchange_body(query, key_rows, value, grad_out, kv_slots):
    devices = lax.axis_size("ctx")
    tokens, probs_shape = exchange_sizes(devices)
    low = lambda *shape: pltpu.VMEM(shape, jnp.bfloat16)
    full = lambda *shape: pltpu.VMEM(shape, jnp.float32)
    anywhere = pl.BlockSpec(memory_space=pl.ANY)
    whole = jax.ShapeDtypeStruct(query.shape, query.dtype)
    by_head = jax.ShapeDtypeStruct((HEADS, BLOCK, HEAD), query.dtype)
    landed = pl.pallas_call(
        functools.partial(exchange_kernel, devices),
        out_shape=(by_head,) * 4,
        in_specs=[anywhere] * 4 + [pl.BlockSpec(memory_space=pltpu.VMEM)],
        out_specs=(anywhere,) * 4,
        scratch_shapes=[low(tokens, HEAD)] * 4
        + [low(HEAD, tokens)] * 4
        + [low(tokens, HEAD)] * 4
        + [full(tokens, HEAD)] * 2
        + [full(devices, tokens), full(*probs_shape), low(4, HEADS, BLOCK, HEAD)]
        + [pltpu.SemaphoreType.DMA((4,))] * 5,
        compiler_params=pltpu.CompilerParams(
            collective_id=0, has_side_effects=True, vmem_limit_bytes=VMEM_BYTES
        ),
    )(query, key_rows, value, grad_out, kv_slots)
    return pl.pallas_call(
        place_kernel,
        out_shape=(whole,) * 4,
        in_specs=[anywhere] * 4,
        out_specs=(anywhere,) * 4,
        scratch_shapes=[pltpu.VMEM((4,) + by_head.shape, query.dtype)]
        + [pltpu.SemaphoreType.DMA((4,))] * 2,
        compiler_params=pltpu.CompilerParams(vmem_limit_bytes=VMEM_BYTES),
    )(*landed)


def fits_exchange(devices, rows):
    if rows != devices * BLOCK or devices % (2 * TILE_H) or not devices // 2 <= HEADS <= devices:
        return False
    _, (groups, keys, queries) = exchange_sizes(devices)
    return groups * keys * queries * 4 <= VMEM_BYTES // 2


def solution(mesh):
    placed = P(("groups", "ctx"), None)

    def chosen(query, key_rows, value, grad_out, kv_slots):
        devices = mesh.shape["ctx"]
        rows = query.shape[0] // mesh.shape["groups"]
        return jax.shard_map(
            exchange_body if fits_exchange(devices, rows) else body,
            mesh=mesh,
            in_specs=(placed,) * 4 + (P(),),
            out_specs=(placed,) * 4,
            check_vma=False,
        )(query, key_rows, value, grad_out, kv_slots)

    return chosen
```

```python
import functools

import jax
import jax.numpy as jnp
from jax import lax
from jax.experimental import pallas as pl
from jax.experimental.pallas import tpu as pltpu
from jax.sharding import PartitionSpec as P

HEADS = 12
HEAD = 128
BLOCK = 128
TILE_H = 4


head_batch = 4
masked_score = -1e30
LOG2_E = 1.4426950408889634
VMEM_BYTES = 63 * 1024 * 1024


def from_behind(value, axis, by):
    count = lax.axis_size(axis)
    return lax.ppermute(value, axis, [(i, (i + by) % count) for i in range(count)])


def neighbour_offsets(devices, blocks, tile_width):
    plane_size = TILE_H * tile_width
    total_slots = devices * blocks
    offset_set = set()
    for plane_step in (0, 1):
        for row_step in (-1, 0, 1):
            for col_step in (-1, 0, 1):
                offset = (plane_step * plane_size + row_step * tile_width + col_step) % total_slots
                target = offset % total_slots // blocks
                if target > devices // 2:
                    target = target - devices
                if target != 0:
                    offset_set.add(target)
    return offset_set


def split_heads(tensor):
    return tensor.reshape(
        tensor.shape[0], HEADS // head_batch, head_batch, tensor.shape[1] // HEADS
    )


def pick_group(tensor, group_index):
    return lax.dynamic_index_in_dim(tensor, group_index, 1, keepdims=False)


def join_heads(stacked):
    return jnp.moveaxis(stacked, 0, 1).reshape(stacked.shape[1], -1)


def apply_mask(scores, block_mask):
    heads_here, row_total, col_total = scores.shape
    row_blocks, col_blocks = block_mask.shape
    shaped = scores.reshape(
        heads_here, row_blocks, row_total // row_blocks, col_blocks, col_total // col_blocks
    )
    shaped = jnp.where(block_mask[None, :, None, :, None], shaped, masked_score)
    return shaped.reshape(heads_here, row_total, col_total)


def forward_group(group_index, queries, keys, values, allowed, scaling):
    query_part = pick_group(queries, group_index)
    key_part = pick_group(keys, group_index)
    value_part = pick_group(values, group_index)
    scores = (
        jnp.einsum("qhd,khd->hqk", query_part, key_part, preferred_element_type=jnp.float32)
        * scaling
    )
    scores = apply_mask(scores, allowed)
    peak_score = jnp.max(scores, axis=2, keepdims=True)
    denominator = jnp.sum(jnp.exp(scores - peak_score), axis=2, keepdims=True)
    log_norm = peak_score + jnp.log(denominator)
    weights = jnp.exp(scores - log_norm).astype(jnp.bfloat16)
    mixed_rows = jnp.einsum("hqk,khd->qhd", weights, value_part, preferred_element_type=jnp.float32)
    return (mixed_rows, log_norm[:, :, 0])


def query_group(
    group_index, queries, keys, values, gradients, log_split, delta_split, allowed, scaling
):
    query_part = pick_group(queries, group_index)
    key_part = pick_group(keys, group_index)
    value_part = pick_group(values, group_index)
    grad_part = pick_group(gradients, group_index)
    log_part = jnp.transpose(pick_group(log_split, group_index))
    delta_part = jnp.transpose(pick_group(delta_split, group_index))
    scores = (
        jnp.einsum("qhd,khd->hqk", query_part, key_part, preferred_element_type=jnp.float32)
        * scaling
    )
    scores = apply_mask(scores, allowed)
    weights = jnp.exp(scores - log_part[:, :, None])
    grad_probs = jnp.einsum(
        "qhd,khd->hqk", grad_part, value_part, preferred_element_type=jnp.float32
    )
    grad_scores = (weights * (grad_probs - delta_part[:, :, None])).astype(jnp.bfloat16)
    return (
        jnp.einsum("hqk,khd->qhd", grad_scores, key_part, preferred_element_type=jnp.float32)
        * scaling
    )


def key_group(
    group_index, keys, values, queries, gradients, log_split, delta_split, back_mask, scaling
):
    key_part = pick_group(keys, group_index)
    value_part = pick_group(values, group_index)
    query_part = pick_group(queries, group_index)
    grad_part = pick_group(gradients, group_index)
    log_part = jnp.transpose(pick_group(log_split, group_index))
    delta_part = jnp.transpose(pick_group(delta_split, group_index))
    scores = (
        jnp.einsum("khd,chd->hkc", key_part, query_part, preferred_element_type=jnp.float32)
        * scaling
    )
    scores = apply_mask(scores, back_mask)
    weights = jnp.exp(scores - log_part[:, None, :])
    grad_probs = jnp.einsum(
        "khd,chd->hkc", value_part, grad_part, preferred_element_type=jnp.float32
    )
    grad_scores = (weights * (grad_probs - delta_part[:, None, :])).astype(jnp.bfloat16)
    grad_values = jnp.einsum(
        "hkc,chd->khd", weights.astype(jnp.bfloat16), grad_part, preferred_element_type=jnp.float32
    )
    grad_keys = (
        jnp.einsum("hkc,chd->khd", grad_scores, query_part, preferred_element_type=jnp.float32)
        * scaling
    )
    return (grad_keys, grad_values)


def body(query, key_rows, value, grad_out, kv_slots):
    devices = lax.axis_size("ctx")
    device_index = lax.axis_index("ctx")
    row_count = query.shape[0]
    blocks = row_count // BLOCK
    tile_width = devices * blocks // (2 * TILE_H)
    offset_set = neighbour_offsets(devices, blocks, tile_width)
    visit_order = sorted(offset_set)
    distances = [0] + visit_order
    local_slots = jnp.arange(blocks, dtype=jnp.int32)
    cand_slots = jnp.concatenate(
        [(device_index + distance) % devices * blocks + local_slots for distance in distances]
    ).astype(jnp.int32)
    own_blocks = device_index * blocks + local_slots
    own_lists = lax.dynamic_slice_in_dim(kv_slots, device_index * blocks, blocks, 0)
    allowed = jnp.any(own_lists[:, :, None] == cand_slots[None, None, :], axis=1)
    cand_lists = jnp.take(kv_slots, cand_slots, axis=0)
    back_mask = jnp.any(cand_lists[None, :, :] == own_blocks[:, None, None], axis=2)
    scaling = HEAD ** (-0.5)
    groups = HEADS // head_batch
    group_ids = jnp.arange(groups)
    arrived = [from_behind((key_rows, value), "ctx", -distance) for distance in visit_order]
    cand_keys = split_heads(jnp.concatenate([key_rows] + [item[0] for item in arrived], axis=0))
    cand_values = split_heads(jnp.concatenate([value] + [item[1] for item in arrived], axis=0))
    queries = split_heads(query)
    mixed_all, norm_all = lax.map(
        lambda group_index: forward_group(
            group_index, queries, cand_keys, cand_values, allowed, scaling
        ),
        group_ids,
    )
    out = join_heads(mixed_all).astype(jnp.bfloat16)
    log_rows = jnp.transpose(norm_all.reshape(HEADS, row_count))
    delta_rows = jnp.sum(
        (grad_out.astype(jnp.float32) * out.astype(jnp.float32)).reshape(row_count, HEADS, -1),
        axis=2,
    )
    gradients = split_heads(grad_out)
    log_split = log_rows.reshape(row_count, groups, head_batch)
    delta_split = delta_rows.reshape(row_count, groups, head_batch)
    query_terms = lax.map(
        lambda group_index: query_group(
            group_index,
            queries,
            cand_keys,
            cand_values,
            gradients,
            log_split,
            delta_split,
            allowed,
            scaling,
        ),
        group_ids,
    )
    grad_query = join_heads(query_terms).astype(jnp.bfloat16)
    returned = [from_behind((query, grad_out), "ctx", -distance) for distance in visit_order]
    cand_queries = jnp.concatenate([query] + [item[0] for item in returned], axis=0)
    cand_grads = jnp.concatenate([grad_out] + [item[1] for item in returned], axis=0)
    row_terms = [from_behind((log_rows, delta_rows), "ctx", -distance) for distance in visit_order]
    cand_log = jnp.concatenate([log_rows] + [item[0] for item in row_terms], axis=0).reshape(
        -1, groups, head_batch
    )
    cand_delta = jnp.concatenate([delta_rows] + [item[1] for item in row_terms], axis=0).reshape(
        -1, groups, head_batch
    )
    own_keys = split_heads(key_rows)
    own_values = split_heads(value)
    split_queries = split_heads(cand_queries)
    split_grads = split_heads(cand_grads)
    key_terms, value_terms = lax.map(
        lambda group_index: key_group(
            group_index,
            own_keys,
            own_values,
            split_queries,
            split_grads,
            cand_log,
            cand_delta,
            back_mask,
            scaling,
        ),
        group_ids,
    )
    grad_key = join_heads(key_terms).astype(jnp.bfloat16)
    grad_value = join_heads(value_terms).astype(jnp.bfloat16)
    return (out, grad_query, grad_key, grad_value)


def head_owner(head, devices):
    chips = devices // 2
    first = (chips - (HEADS - chips)) // 2
    return jnp.where(head < chips, 2 * head, 2 * (head - chips + first) + 1)


def head_of(device, devices):
    chips = devices // 2
    extra = HEADS - chips
    first = (chips - extra) // 2
    chip = device // 2
    odd = device % 2
    inside = (chip >= first) & (chip < first + extra)
    second = jnp.where(inside, chips + chip - first, -1)
    return jnp.where(odd == 0, jnp.where(chip < HEADS, chip, -1), second)


def exchange_kernel(
    devices,
    query_ref,
    key_ref,
    value_ref,
    grad_ref,
    slots_ref,
    out_ref,
    dq_ref,
    dk_ref,
    dv_ref,
    q_all,
    k_all,
    v_all,
    g_all,
    kt_all,
    vt_all,
    gt_all,
    ot_all,
    o_all,
    dq_all,
    dk_all,
    dv_all,
    dk_sum,
    dv_sum,
    bias,
    probs,
    low_probs,
    staged,
    stage_sem,
    in_send,
    in_recv,
    out_send,
    out_recv,
):
    me = lax.axis_index("ctx")
    my_head = head_of(me, devices)
    owns = my_head >= 0
    tokens = devices * BLOCK
    width = devices // (2 * TILE_H)
    row_tokens = width * BLOCK
    plane_tokens = tokens // 2
    scaling = HEAD ** (-0.5)

    sources = (key_ref, query_ref, value_ref, grad_ref)
    landings = (k_all, q_all, v_all, g_all)
    own_rows = pl.ds(pl.multiple_of(me * BLOCK, BLOCK), BLOCK)
    barrier = pltpu.get_barrier_semaphore()
    for step in range(1, devices):
        pl.semaphore_signal(
            barrier,
            inc=1,
            device_id={"ctx": lax.rem(me + step, devices)},
            device_id_type=pl.DeviceIdType.MESH,
        )
    for index in range(4):
        for head in range(HEADS):
            pltpu.make_async_copy(
                sources[index].at[:, head * HEAD : (head + 1) * HEAD],
                staged.at[index, head],
                stage_sem.at[index],
            ).start()

    pl.semaphore_wait(barrier, devices - 1)

    half = me // (devices // 2)
    chips = devices // 2
    pairs = HEADS // 2

    def send_inputs(index):
        source, landing = sources[index], landings[index]
        pltpu.make_async_copy(staged.at[index], staged.at[index], stage_sem.at[index]).wait()

        def one(step, carry):
            place = lax.rem(me + step, pairs)
            for side in (1 - half, half):
                head = jnp.where(
                    place < chips // 2,
                    place + side * (chips // 2),
                    chips + place - chips // 2 + side * ((HEADS - chips) // 2),
                )
                owner = head_owner(head, devices)
                columns = pl.ds(pl.multiple_of(head * HEAD, HEAD), HEAD)

                @pl.when(owner != me)
                def _():
                    pltpu.make_async_remote_copy(
                        src_ref=staged.at[index, head],
                        dst_ref=landing.at[own_rows, :],
                        send_sem=in_send.at[index],
                        recv_sem=in_recv.at[index],
                        device_id={"ctx": owner},
                        device_id_type=pl.DeviceIdType.MESH,
                    ).start()

                @pl.when(owner == me)
                def _():
                    pltpu.make_async_copy(
                        source.at[:, columns], landing.at[own_rows, :], in_recv.at[index]
                    ).start()

            return carry

        lax.fori_loop(0, pairs, one, 0)

    for index in range(4):
        send_inputs(index)

    def arrived(index):
        pltpu.make_async_copy(landings[index], landings[index], in_recv.at[index]).wait()

    results = (o_all, dq_all, dk_all, dv_all)
    targets = (out_ref, dq_ref, dk_ref, dv_ref)

    def send_rows(indices, rows_here):
        for index in indices:
            result, target = results[index], targets[index]
            for column in range(width):
                for side in (1 - half, half):
                    for row in rows_here:
                        other = side * (devices // 2) + row * width + column
                        rows = pl.ds(pl.multiple_of(other * BLOCK, BLOCK), BLOCK)

                        @pl.when(other != me)
                        def _():
                            pltpu.make_async_remote_copy(
                                src_ref=result.at[rows, :],
                                dst_ref=target.at[my_head],
                                send_sem=out_send.at[index],
                                recv_sem=out_recv.at[index],
                                device_id={"ctx": other},
                                device_id_type=pl.DeviceIdType.MESH,
                            ).start()

                        @pl.when(other == me)
                        def _():
                            pltpu.make_async_copy(
                                result.at[rows, :], target.at[my_head], out_recv.at[index]
                            ).start()

    def dot(left, right):
        return jnp.dot(left, right, preferred_element_type=jnp.float32)

    def dot_nt(left, right):
        return lax.dot_general(
            left, right, (((1,), (1,)), ((), ())), preferred_element_type=jnp.float32
        )

    def flip(ref, target):
        for start in range(0, tokens, row_tokens):
            part = ref[start : start + row_tokens, :].astype(jnp.float32)
            target[:, start : start + row_tokens] = jnp.transpose(part).astype(target.dtype)

    groups = []
    for row in range(TILE_H):
        low, high = max(row - 1, 0), min(row + 1, TILE_H - 1)
        count = (high + 1 - low) * row_tokens
        for plane in range(2):
            groups.append(
                (
                    plane * plane_tokens + row * row_tokens,
                    [(0, low * row_tokens), (count, plane_tokens + low * row_tokens)],
                    count,
                )
            )

    def finish_keys(rows_here):
        for plane in range(2):
            start = plane * plane_tokens + rows_here[0] * row_tokens
            span = slice(start, start + len(rows_here) * row_tokens)
            dv_all[span, :] = dv_sum[span, :].astype(jnp.bfloat16)
            dk_all[span, :] = (dk_sum[span, :] * scaling).astype(jnp.bfloat16)
        send_rows((3, 2), rows_here)

    @pl.when(owns)
    def _():
        for block in range(devices):
            listed = slots_ref[block : block + 1, :]
            ids = lax.broadcasted_iota(jnp.int32, (devices, listed.shape[1]), 0)
            hit = jnp.where(ids == listed, 0.0, -1e30)
            best = jnp.max(hit, axis=1, keepdims=True)
            bias[:, block * BLOCK : (block + 1) * BLOCK] = jnp.broadcast_to(best, (devices, BLOCK))
        dk_sum[...] = jnp.zeros_like(dk_sum)
        dv_sum[...] = jnp.zeros_like(dv_sum)

        arrived(0)
        arrived(1)
        flip(k_all, kt_all)
        for index, (start, ranges, count) in enumerate(groups):
            queries = q_all[start : start + row_tokens, :]
            scores = []
            for offset, first in ranges:
                part = dot_nt(k_all[first : first + count, :], queries)
                blocks = count // BLOCK
                shift = bias[first // BLOCK : first // BLOCK + blocks, start : start + row_tokens]
                part = part.reshape(blocks, BLOCK, row_tokens) + shift[:, None, :]
                scores.append(part.reshape(count, row_tokens))
            peak = jnp.maximum(
                jnp.max(scores[0], axis=0, keepdims=True), jnp.max(scores[1], axis=0, keepdims=True)
            )
            powers = [jnp.exp2((part - peak) * (scaling * LOG2_E)) for part in scores]
            total = jnp.sum(powers[0], axis=0, keepdims=True) + jnp.sum(
                powers[1], axis=0, keepdims=True
            )
            inverse = 1.0 / total
            for (offset, first), part in zip(ranges, powers):
                part = part * inverse
                probs[index, offset : offset + count, :] = part
                low_probs[index, offset : offset + count, :] = part.astype(jnp.bfloat16)

        arrived(2)
        flip(v_all, vt_all)
        for index, (start, ranges, count) in enumerate(groups):
            mixed = jnp.zeros((HEAD, row_tokens), jnp.float32)
            for offset, first in ranges:
                weights = low_probs[index, offset : offset + count, :]
                mixed += dot(vt_all[:, first : first + count], weights)
            ot_all[:, start : start + row_tokens] = mixed.astype(jnp.bfloat16)
            o_all[start : start + row_tokens, :] = jnp.transpose(mixed).astype(jnp.bfloat16)
            if index % 4 == 3:
                send_rows((0,), (index // 2 - 1, index // 2))

        arrived(3)
        flip(g_all, gt_all)
        for index, (start, ranges, count) in enumerate(groups):
            span = slice(start, start + row_tokens)
            delta = jnp.sum(
                gt_all[:, span].astype(jnp.float32) * ot_all[:, span].astype(jnp.float32),
                axis=0,
                keepdims=True,
            )
            grads = g_all[span, :]
            queries = q_all[span, :]
            turned = jnp.zeros((HEAD, row_tokens), jnp.float32)
            for offset, first in ranges:
                keys = slice(first, first + count)
                exact = probs[index, offset : offset + count, :]
                dv_sum[keys, :] += dot(low_probs[index, offset : offset + count, :], grads)
                product = dot_nt(v_all[keys, :], grads)
                slopes = (exact * (product - delta)).astype(jnp.bfloat16)
                turned += dot(kt_all[:, keys], slopes)
                dk_sum[keys, :] += dot(slopes, queries)
            dq_all[span, :] = jnp.transpose(turned * scaling).astype(jnp.bfloat16)
            if index % 4 == 3:
                send_rows((1,), (index // 2 - 1, index // 2))
            if index % 4 == 1 and index > 1:
                finish_keys((index // 2 - 2, index // 2 - 1))
        finish_keys((TILE_H - 2, TILE_H - 1))

        for index in range(4):
            sent = staged.at[index, pl.ds(0, HEADS - 1)]
            pltpu.make_async_copy(sent, sent, in_send.at[index]).wait()
            sent = results[index].at[: (devices - 1) * BLOCK, :]
            pltpu.make_async_copy(sent, sent, out_send.at[index]).wait()

    @pl.when(jnp.logical_not(owns))
    def _():
        for index in range(4):
            pltpu.make_async_copy(staged.at[index], staged.at[index], in_send.at[index]).wait()

    for index in range(4):
        pltpu.make_async_copy(targets[index], targets[index], out_recv.at[index]).wait()


def place_kernel(*refs):
    sources, targets, held, in_sem, out_sem = refs[:4], refs[4:8], refs[8], refs[9], refs[10]
    loads = [
        pltpu.make_async_copy(sources[index], held.at[index], in_sem.at[index])
        for index in range(4)
    ]
    for load in loads:
        load.start()
    for index, load in enumerate(loads):
        load.wait()
        for head in range(HEADS):
            pltpu.make_async_copy(
                held.at[index, head],
                targets[index].at[:, head * HEAD : (head + 1) * HEAD],
                out_sem.at[index],
            ).start()
    for index in range(4):
        pltpu.make_async_copy(held.at[index], held.at[index], out_sem.at[index]).wait()


def exchange_sizes(devices):
    tokens = devices * BLOCK
    row_tokens = tokens // (2 * TILE_H)
    return tokens, (2 * TILE_H, 6 * row_tokens, row_tokens)


def exchange_body(query, key_rows, value, grad_out, kv_slots):
    devices = lax.axis_size("ctx")
    tokens, probs_shape = exchange_sizes(devices)
    low = lambda *shape: pltpu.VMEM(shape, jnp.bfloat16)
    full = lambda *shape: pltpu.VMEM(shape, jnp.float32)
    anywhere = pl.BlockSpec(memory_space=pl.ANY)
    whole = jax.ShapeDtypeStruct(query.shape, query.dtype)
    by_head = jax.ShapeDtypeStruct((HEADS, BLOCK, HEAD), query.dtype)
    landed = pl.pallas_call(
        functools.partial(exchange_kernel, devices),
        out_shape=(by_head,) * 4,
        in_specs=[anywhere] * 4 + [pl.BlockSpec(memory_space=pltpu.VMEM)],
        out_specs=(anywhere,) * 4,
        scratch_shapes=[low(tokens, HEAD)] * 4
        + [low(HEAD, tokens)] * 4
        + [low(tokens, HEAD)] * 4
        + [full(tokens, HEAD)] * 2
        + [full(devices, tokens), full(*probs_shape), low(*probs_shape), low(4, HEADS, BLOCK, HEAD)]
        + [pltpu.SemaphoreType.DMA((4,))] * 5,
        compiler_params=pltpu.CompilerParams(
            collective_id=0, has_side_effects=True, vmem_limit_bytes=VMEM_BYTES
        ),
    )(query, key_rows, value, grad_out, kv_slots)
    return pl.pallas_call(
        place_kernel,
        out_shape=(whole,) * 4,
        in_specs=[anywhere] * 4,
        out_specs=(anywhere,) * 4,
        scratch_shapes=[pltpu.VMEM((4,) + by_head.shape, query.dtype)]
        + [pltpu.SemaphoreType.DMA((4,))] * 2,
        compiler_params=pltpu.CompilerParams(vmem_limit_bytes=VMEM_BYTES),
    )(*landed)


def fits_exchange(devices, rows):
    if rows != devices * BLOCK or devices % (2 * TILE_H) or not devices // 2 <= HEADS <= devices:
        return False
    _, (groups, keys, queries) = exchange_sizes(devices)
    return groups * keys * queries * 4 <= VMEM_BYTES // 2


def solution(mesh):
    placed = P(("groups", "ctx"), None)

    def chosen(query, key_rows, value, grad_out, kv_slots):
        devices = mesh.shape["ctx"]
        rows = query.shape[0] // mesh.shape["groups"]
        return jax.shard_map(
            exchange_body if fits_exchange(devices, rows) else body,
            mesh=mesh,
            in_specs=(placed,) * 4 + (P(),),
            out_specs=(placed,) * 4,
            check_vma=False,
        )(query, key_rows, value, grad_out, kv_slots)

    return chosen
```
